32 devices in a mesh: track: 8 (over z, x), tm: 4 (over y, core).
Axes of the slice: x: 2, y: 2, z: 4, core: 2. Of those that a mesh axis runs over, the one named last changes fastest.
Arguments:
- positions: float32 [3, 8, 3072], P(None, 'tm', 'track'), may hold values from -6 to 6
- embeddings: float32 [8, 128, 3072], P('tm', None, 'track'), may hold values from -6 to 6
- visible: int32 [8, 3072], P('tm', 'track'), may hold values 0 or 1
Outputs:
- grad_positions: float32 [3, 8, 3072], P(None, 'tm', 'track')
- grad_embeddings: float32 [8, 128, 3072], P('tm', None, 'track')
- mean_loss: float32 [], replicated
The draws below stay inside these ranges and needn't reach their ends.
All inputs are finite; a program needn't handle non-finite values. No bound on the sum of `visible` on one device may be relied on, other than what follows from the above.
Results may differ from the reference program's by a relative error of at most 0.00014.
Values sent between devices are 32-bit elements; how exact they have to be, the bound alone decides.
No kernel may reach another device: no remote copies, remote signals or barrier semaphores. Data moves between devices by JAX's collectives and lax.ppermute only.
A program may use at most 128 MiB of HBM per device.

```python
import math
import jax
import jax.numpy as jnp
from jax import lax

EMB = 128
TRACKS = 3072
FRAMES = 8


def place_ends(entries, own_key, low, largest):
    spot = [jax.random.randint(jax.random.fold_in(own_key, axis), (), 0, length) for axis, length in enumerate(entries.shape)]
    widest = entries.shape.index(max(entries.shape))
    next_to = spot[:widest] + [(spot[widest] + 1) % entries.shape[widest]] + spot[widest + 1:]
    return entries.at[tuple(spot)].set(low).at[tuple(next_to)].set(largest)


def level_of(stream_key, extent, pieces, least, largest):
    gain = 1.0
    for axis_at, blocks in pieces:
        draws = jax.random.uniform(jax.random.fold_in(jax.random.fold_in(stream_key, 6), axis_at), (blocks,), jnp.float32, least / len(pieces), largest / len(pieces))
        gain = gain * jnp.repeat(jnp.exp(draws), extent[axis_at] // blocks).reshape((-1,) + (1,) * (len(extent) - 1 - axis_at))
    return gain


def normal_values(rng, dims, scale, reach, split=(), dtype=jnp.bfloat16):
    drawn = scale * jax.random.normal(rng, dims, jnp.float32)
    if split:
        drawn = drawn * level_of(rng, dims, split, -0.22, 0.18)
    return jnp.clip(drawn, -reach, reach).astype(dtype)


def setup_inputs(seed: int = 0) -> dict:
    seeds = jax.random.split(jax.random.key(seed), 4)
    positions = normal_values(seeds[0], (3, FRAMES, TRACKS), 1.0, 6.0, ((1, 4), (2, 8)), jnp.float32)
    embeddings = normal_values(seeds[1], (FRAMES, EMB, TRACKS), 1.0, 6.0, ((0, 4), (2, 8)), jnp.float32)
    visible = place_ends((jax.random.randint(seeds[2], (FRAMES, TRACKS), 0, 4) < 3).astype(jnp.int32), jax.random.fold_in(seeds[2], 1), 0, 1)
    return {"positions": positions, "embeddings": embeddings, "visible": visible}


rigidity = 4.0
highest = lax.Precision.HIGHEST

def tile_terms(pos_a, mask_a, emb_a, pos_b, mask_b, emb_b, weight_scale):
    inv_root = 1.0 / math.sqrt(emb_a.shape[1])
    offset = pos_a[:, :, :, None] - pos_b[:, :, None, :]
    distance = jnp.sqrt(lax.optimization_barrier(jnp.sum(offset * offset, axis=0)) + 1.0)
    change = distance[1:] - distance[:-1]
    both_seen = mask_a[:, :, None] * mask_b[:, None, :]
    seen_pair = both_seen[1:] * both_seen[:-1]
    logits = jnp.einsum('fei,fej->fij', emb_a, emb_b, precision=highest) * inv_root
    affinity = jax.nn.sigmoid(logits)
    squared = seen_pair * change * change
    energy = jnp.sum(affinity * squared)
    grad_change = 2.0 * weight_scale * affinity * seen_pair * change
    padding = jnp.zeros_like(grad_change[:1])
    grad_dist = jnp.concatenate([padding, grad_change], 0) - jnp.concatenate([grad_change, padding], 0)
    scaled = (grad_dist / distance)[None] * offset
    grad_pos_a = lax.optimization_barrier(jnp.sum(scaled, axis=3))
    grad_pos_b = -lax.optimization_barrier(jnp.sum(scaled, axis=2))
    grad_logit = weight_scale * squared * affinity * (1.0 - affinity) * inv_root
    grad_emb_a = jnp.einsum('fij,fej->fei', grad_logit, emb_b, precision=highest)
    grad_emb_b = jnp.einsum('fij,fei->fej', grad_logit, emb_a, precision=highest)
    return (energy, grad_pos_a, grad_emb_a, grad_pos_b, grad_emb_b)

def reference(positions, embeddings, visible):
    frames = positions.shape[1]
    tracks = positions.shape[2]
    width = embeddings.shape[1]
    weight_scale = rigidity / math.sqrt(tracks)
    seen_mask = visible.astype(jnp.float32)
    tile_size = min(256, tracks)
    tile_count = tracks // tile_size
    pos_blocks = positions.reshape(3, frames, tile_count, tile_size).transpose(2, 0, 1, 3)
    mask_blocks = seen_mask.reshape(frames, tile_count, tile_size).transpose(1, 0, 2)
    emb_blocks = embeddings[:frames - 1].reshape(frames - 1, width, tile_count, tile_size).transpose(2, 0, 1, 3)

    def per_row(inputs):
        pos_a, mask_a, emb_a = inputs

        def advance(totals, others):
            pos_b, mask_b, emb_b = others
            energy, grad_pos_a, grad_emb_a, unused_pos, unused_emb = tile_terms(pos_a, mask_a, emb_a, pos_b, mask_b, emb_b, weight_scale)
            return ((totals[0] + energy, totals[1] + grad_pos_a, totals[2] + grad_emb_a), None)
        initial = (jnp.zeros((), jnp.float32), jnp.zeros_like(pos_a), jnp.zeros_like(emb_a))
        result, unused = lax.scan(advance, initial, (pos_blocks, mask_blocks, emb_blocks))
        return result
    energies, grad_pos, grad_emb = lax.map(per_row, (pos_blocks, mask_blocks, emb_blocks))
    grad_positions = grad_pos.transpose(1, 2, 0, 3).reshape(3, frames, tracks)
    grad_emb = grad_emb.transpose(1, 2, 0, 3).reshape(frames - 1, width, tracks)
    grad_embeddings = jnp.concatenate([grad_emb, jnp.zeros((1, width, tracks), jnp.float32)], 0)
    total = 0.5 * jnp.sum(energies)
    mean_loss = total / (tracks * (tracks - 1) / 2.0 * (frames - 1))
    return (grad_positions, grad_embeddings, mean_loss)
```

```python
import functools
import math

import jax
import jax.numpy as jnp
from jax import lax
from jax.experimental import pallas as pl
from jax.experimental.pallas import tpu as pltpu
from jax.sharding import PartitionSpec as P

f32 = jnp.float32
bf16 = jnp.bfloat16
rigidity = 4.0
AXES = ("track", "tm")
COMPS = 7


def split(values):
    high = values.astype(bf16)
    return high, (values - high.astype(f32)).astype(bf16)


def pair_kernel(own_n, col_n, chunk, strip, rows, final, weight_scale, *refs):
    refs = list(refs)

    def take(count):
        taken = refs[:count]
        del refs[:count]
        return taken

    own_emb, own_pts, col_emb, col_pts = take(own_n), take(own_n), take(col_n), take(col_n)
    prev = take(2) if final[0] else None
    outs = take(own_n + 1 if final[1] else 2)
    weights, lhs, emb_split, points, logits, g_high, g_low, sums, own, grad = refs
    emb, width = own_emb[0].shape
    own_size, col_size = width * own_n, width * col_n
    inv_root = 1.0 / math.sqrt(emb)
    for a in range(own_n):
        at = slice(a * width, (a + 1) * width)
        high, low = split(own_emb[a][...] * (0.5 * inv_root))
        weights[0:emb, at] = high
        weights[emb : 2 * emb, at] = low
        weights[2 * emb : 3 * emb, at] = high
        own[:, at] = own_pts[a][...]
    for b in range(col_n):
        at = slice(b * width, (b + 1) * width)
        values = col_emb[b][...]
        high, low = split(values)
        emb_split[0:emb, at] = high
        emb_split[emb : 2 * emb, at] = low
        high, low = split(values.T)
        lhs[at, 0:emb] = high
        lhs[at, emb : 2 * emb] = high
        lhs[at, 2 * emb : 3 * emb] = low
        flipped = col_pts[b][...].T
        for c in range(COMPS):
            points[c, at, :] = jnp.broadcast_to(flipped[:, c : c + 1], (width, 128))
    sums[...] = jnp.zeros_like(sums)
    if prev is None:
        grad[...] = jnp.zeros_like(grad)
    else:
        grad[...] = prev[0][...]

    def fold(values):
        return values.reshape(rows // 8, 8, strip).sum(0)

    def step(n, carry):
        first = pl.multiple_of(n * chunk, chunk)
        logits[...] = jnp.dot(lhs[pl.ds(first, chunk), :], weights[...], preferred_element_type=f32)
        for i in range(0, own_size, strip):
            at = slice(i, i + strip)
            mine = [jnp.broadcast_to(own[c : c + 1, at], (rows, strip)) for c in range(6)]
            total = [sums[k, :, at] for k in range(COMPS)]
            for b in range(0, chunk, rows):
                theirs = [
                    jnp.concatenate([points[c, pl.ds(first + b, rows), :]] * (strip // 128), 1)
                    for c in range(COMPS)
                ]
                off = [mine[c] - theirs[c] for c in range(6)]
                sq0 = off[0] * off[0] + off[1] * off[1] + off[2] * off[2] + 1.0
                sq1 = off[3] * off[3] + off[4] * off[4] + off[5] * off[5] + 1.0
                inv0 = lax.rsqrt(sq0)
                inv1 = lax.rsqrt(sq1)
                change = sq1 * inv1 - sq0 * inv0
                tanh = jnp.tanh(logits[b : b + rows, at])
                pull = (change + change * tanh) * theirs[6]
                energy = pull * change
                high, low = split(energy - energy * tanh)
                g_high[b : b + rows, at] = high
                g_low[b : b + rows, at] = low
                w0 = pull * inv0
                w1 = pull * inv1
                for c in range(3):
                    total[c] = total[c] + fold(w0 * off[c])
                    total[3 + c] = total[3 + c] + fold(w1 * off[3 + c])
                total[6] = total[6] + fold(energy)
            for k in range(COMPS):
                sums[k, :, at] = total[k]
        both = jnp.dot(emb_split[:, pl.ds(first, chunk)], g_high[...], preferred_element_type=f32)
        rest = jnp.dot(emb_split[0:emb, pl.ds(first, chunk)], g_low[...], preferred_element_type=f32)
        grad[...] += both[:emb] + both[emb:] + rest
        return carry

    lax.fori_loop(0, col_size // chunk, step, 0)
    if not final[1]:
        outs[0][...] = grad[...]
        for k in range(COMPS):
            row = jnp.sum(sums[k], axis=0, keepdims=True)
            outs[1][k : k + 1, :] = row if prev is None else row + prev[1][k : k + 1, :]
        outs[1][COMPS:8, :] = jnp.zeros((8 - COMPS, own_size), f32)
        return
    seen = own[6:7, :] * weight_scale
    scale = seen * (0.25 * inv_root)
    lines = []
    for k in range(COMPS):
        row = jnp.sum(sums[k], axis=0, keepdims=True)
        lines.append(row if prev is None else row + prev[1][k : k + 1, :])
    for a in range(own_n):
        at = slice(a * width, (a + 1) * width)
        outs[a][0:emb, :] = grad[:, at] * scale[:, at]
        for c in range(3):
            outs[a][emb + c : emb + c + 1, :] = -lines[c][:, at] * seen[:, at]
            outs[a][emb + 3 + c : emb + 4 + c, :] = lines[3 + c][:, at] * seen[:, at]
        outs[a][emb + 6 : emb + 8, :] = jnp.zeros((2, width), f32)
    loss = jnp.sum(lines[6] * own[6:7, :], axis=1, keepdims=True)
    outs[own_n][...] = jnp.broadcast_to(loss, outs[own_n].shape)


def pair_terms(own_emb, own_pts, col_emb, col_pts, prev, last, peers, weight_scale):
    own_n, col_n = len(own_emb), len(col_emb)
    emb, width = own_emb[0].shape
    own_size, col_size = width * own_n, width * col_n
    chunk = strip = 256
    if col_size % chunk or own_size % strip:
        chunk = strip = 128
    if last:
        out_shape = [jax.ShapeDtypeStruct((emb + 8, width), f32)] * own_n
        out_shape.append(jax.ShapeDtypeStruct((peers, 128), f32))
    else:
        out_shape = [
            jax.ShapeDtypeStruct((emb, own_size), f32),
            jax.ShapeDtypeStruct((8, own_size), f32),
        ]
    extra = [] if prev is None else list(prev)
    pairs = own_size * col_size
    return pl.pallas_call(
        functools.partial(
            pair_kernel, own_n, col_n, chunk, strip, 32, (prev is not None, last), weight_scale
        ),
        out_shape=out_shape,
        scratch_shapes=[
            pltpu.VMEM((3 * emb, own_size), bf16),
            pltpu.VMEM((col_size, 3 * emb), bf16),
            pltpu.VMEM((2 * emb, col_size), bf16),
            pltpu.VMEM((COMPS, col_size, 128), f32),
            pltpu.VMEM((chunk, own_size), f32),
            pltpu.VMEM((chunk, own_size), bf16),
            pltpu.VMEM((chunk, own_size), bf16),
            pltpu.VMEM((COMPS, 8, own_size), f32),
            pltpu.VMEM((8, own_size), f32),
            pltpu.VMEM((emb, own_size), f32),
        ],
        compiler_params=pltpu.CompilerParams(vmem_limit_bytes=40 * 2**20),
        cost_estimate=pl.CostEstimate(
            flops=pairs * 12 * emb, bytes_accessed=pairs * 4, transcendentals=3 * pairs
        ),
    )(*own_emb, *own_pts, *col_emb, *col_pts, *extra)


def pick(options, index):
    chosen = options[0]
    for n in range(1, len(options)):
        chosen = jnp.where(index == n, options[n], chosen)
    return chosen


def on_device(positions, embeddings, visible):
    frames_local, emb, width = embeddings.shape
    track_n, tm_n = lax.axis_size("track"), lax.axis_size("tm")
    tracks, frames = width * track_n, frames_local * tm_n
    weight_scale = rigidity / math.sqrt(tracks)
    team = 2 * frames_local
    teams = track_n // team

    def homes():
        for track in range(track_n):
            for tm in range(tm_n):
                yield track, tm

    def worker(track, tm, turn, shift):
        crew, member = divmod(track, team)
        frame = (turn + member) % frames_local
        core = tm % 2
        to_track = (crew + shift) % teams * team + core * frames_local + frame
        return to_track * tm_n + (tm - core + member // frames_local), frame

    def outward(turn, shift):
        return [(t * tm_n + m, worker(t, m, turn, shift)[0]) for t, m in homes()]

    def inward(turn):
        return [(worker(t, m, turn, 0)[0], t * tm_n + m) for t, m in homes()]

    def inward_next(turn):
        pairs = []
        for t, m in homes():
            at, frame = worker(t, m, turn, 0)
            if frame == frames_local - 1 and m + 1 < tm_n:
                pairs.append((at, t * tm_n + m + 1))
        return pairs

    swap = [(t * tm_n + m, t * tm_n + (m ^ 1)) for t, m in homes()]
    member = lax.rem(lax.axis_index("track"), team)
    turns = range(frames_local)

    frame_of = [lax.rem(member + turn, frames_local) for turn in turns]
    sent = [pick([embeddings[k] for k in turns], frame_of[turn]) for turn in turns]
    arrived = [
        [lax.ppermute(sent[turn], AXES, outward(turn, shift)) for turn in turns]
        for shift in range(teams)
    ]

    seen = visible.astype(f32)
    rows = jnp.concatenate([positions, seen[None]], 0)
    following = lax.ppermute(rows[:, 0], "tm", [(i, i - 1) for i in range(1, tm_n)])
    rows = jnp.concatenate([rows, following[:, None]], 1)
    points = []
    for k in turns:
        points.append(
            jnp.concatenate(
                [
                    rows[:3, k],
                    rows[:3, k + 1],
                    rows[3:, k] * rows[3:, k + 1],
                    jnp.zeros((1, width), f32),
                ],
                0,
            )
        )
    sent_pts = [pick(points, frame_of[turn]) for turn in turns]
    arrived_pts = [
        [lax.ppermute(sent_pts[turn], AXES, outward(turn, shift)) for turn in turns]
        for shift in range(teams)
    ]
    beside = [[lax.ppermute(v, AXES, swap) for v in group] for group in arrived]
    beside_pts = [[lax.ppermute(v, AXES, swap) for v in group] for group in arrived_pts]

    own_emb, own_pts = arrived[0], arrived_pts[0]
    stages = [(arrived[0] + beside[0], arrived_pts[0] + beside_pts[0])]
    for shift in range(1, teams):
        for turn in turns:
            stages.append(
                (
                    [arrived[shift][turn], beside[shift][turn]],
                    [arrived_pts[shift][turn], beside_pts[shift][turn]],
                )
            )
    totals = None
    for n, (col_emb, col_pts) in enumerate(stages):
        totals = pair_terms(
            own_emb,
            own_pts,
            col_emb,
            col_pts,
            totals,
            n == len(stages) - 1,
            track_n * tm_n,
            weight_scale,
        )

    back = [lax.ppermute(totals[turn], AXES, inward(turn)) for turn in turns]
    late = [lax.ppermute(totals[turn][emb:], AXES, inward_next(turn)) for turn in turns]
    shares = lax.all_to_all(totals[frames_local], AXES, 0, 0, tiled=True)
    total = jnp.sum(shares[:, :1]) * 0.25
    mean_loss = total / (tracks * (tracks - 1) / 2.0 * (frames - 1))

    of_frame = [
        pick(back, lax.rem(k - member + team * frames_local, frames_local)) for k in turns
    ]
    grad_emb = jnp.stack([v[:emb] for v in of_frame])
    from_before = sum(v[3:6] for v in late)
    grad_pos = []
    for k in turns:
        extra = from_before if k == 0 else of_frame[k - 1][emb + 3 : emb + 6]
        grad_pos.append(of_frame[k][emb : emb + 3] + extra)
    return (jnp.stack(grad_pos, 1), grad_emb, mean_loss)


def solution(mesh):
    in_specs = (P(None, "tm", "track"), P("tm", None, "track"), P("tm", "track"))
    out_specs = (P(None, "tm", "track"), P("tm", None, "track"), P())
    return jax.shard_map(
        on_device, mesh=mesh, in_specs=in_specs, out_specs=out_specs, check_vma=False
    )
```

```python
import functools
import math

import jax
import jax.numpy as jnp
from jax import lax
from jax.experimental import pallas as pl
from jax.experimental.pallas import tpu as pltpu
from jax.sharding import PartitionSpec as P

f32 = jnp.float32
bf16 = jnp.bfloat16
rigidity = 4.0
AXES = ("track", "tm")
COMPS = 7


def split(values):
    high = values.astype(bf16)
    return high, (values - high.astype(f32)).astype(bf16)


def pair_kernel(own_n, col_n, chunk, strip, rows, final, weight_scale, *refs):
    refs = list(refs)

    def take(count):
        taken = refs[:count]
        del refs[:count]
        return taken

    own_blocks, col_blocks = take(own_n), take(col_n)
    prev = take(2) if final[0] else None
    outs = take(own_n + 1 if final[1] else 2)
    weights, lhs, emb_split, points, logits, g_high, g_low, sums, own, grad = refs
    emb, width = own_blocks[0].shape[0] - 8, own_blocks[0].shape[1]
    own_size, col_size = width * own_n, width * col_n
    inv_root = 1.0 / math.sqrt(emb)
    for a in range(own_n):
        at = slice(a * width, (a + 1) * width)
        high, low = split(own_blocks[a][0:emb, :] * (0.5 * inv_root))
        weights[0:emb, at] = high
        weights[emb : 2 * emb, at] = low
        weights[2 * emb : 3 * emb, at] = high
        own[:, at] = own_blocks[a][emb : emb + 8, :]
    for b in range(col_n):
        at = slice(b * width, (b + 1) * width)
        values = col_blocks[b][0:emb, :]
        high, low = split(values)
        emb_split[0:emb, at] = high
        emb_split[emb : 2 * emb, at] = low
        high, low = split(values.T)
        lhs[at, 0:emb] = high
        lhs[at, emb : 2 * emb] = high
        lhs[at, 2 * emb : 3 * emb] = low
        flipped = col_blocks[b][emb : emb + 8, :].T
        for c in range(COMPS):
            points[c, at, :] = jnp.broadcast_to(flipped[:, c : c + 1], (width, 128))
    sums[...] = jnp.zeros_like(sums)
    if prev is None:
        grad[...] = jnp.zeros_like(grad)
    else:
        grad[...] = prev[0][...]

    def fold(values):
        return values.reshape(rows // 8, 8, strip).sum(0)

    def step(n, carry):
        first = pl.multiple_of(n * chunk, chunk)
        logits[...] = jnp.dot(lhs[pl.ds(first, chunk), :], weights[...], preferred_element_type=f32)
        for i in range(0, own_size, strip):
            at = slice(i, i + strip)
            mine = [jnp.broadcast_to(own[c : c + 1, at], (rows, strip)) for c in range(6)]
            total = [sums[k, :, at] for k in range(COMPS)]
            for b in range(0, chunk, rows):
                theirs = [
                    jnp.concatenate([points[c, pl.ds(first + b, rows), :]] * (strip // 128), 1)
                    for c in range(COMPS)
                ]
                off = [mine[c] - theirs[c] for c in range(6)]
                sq0 = off[0] * off[0] + off[1] * off[1] + off[2] * off[2] + 1.0
                sq1 = off[3] * off[3] + off[4] * off[4] + off[5] * off[5] + 1.0
                inv0 = lax.rsqrt(sq0)
                inv1 = lax.rsqrt(sq1)
                change = sq1 * inv1 - sq0 * inv0
                tanh = jnp.tanh(logits[b : b + rows, at])
                pull = (change + change * tanh) * theirs[6]
                energy = pull * change
                high, low = split(energy - energy * tanh)
                g_high[b : b + rows, at] = high
                g_low[b : b + rows, at] = low
                w0 = pull * inv0
                w1 = pull * inv1
                for c in range(3):
                    total[c] = total[c] + fold(w0 * off[c])
                    total[3 + c] = total[3 + c] + fold(w1 * off[3 + c])
                total[6] = total[6] + fold(energy)
            for k in range(COMPS):
                sums[k, :, at] = total[k]
        both = jnp.dot(emb_split[:, pl.ds(first, chunk)], g_high[...], preferred_element_type=f32)
        rest = jnp.dot(emb_split[0:emb, pl.ds(first, chunk)], g_low[...], preferred_element_type=f32)
        grad[...] += both[:emb] + both[emb:] + rest
        return carry

    lax.fori_loop(0, col_size // chunk, step, 0)
    if not final[1]:
        outs[0][...] = grad[...]
        for k in range(COMPS):
            row = jnp.sum(sums[k], axis=0, keepdims=True)
            outs[1][k : k + 1, :] = row if prev is None else row + prev[1][k : k + 1, :]
        outs[1][COMPS:8, :] = jnp.zeros((8 - COMPS, own_size), f32)
        return
    seen = own[6:7, :] * weight_scale
    scale = seen * (0.25 * inv_root)
    lines = []
    for k in range(COMPS):
        row = jnp.sum(sums[k], axis=0, keepdims=True)
        lines.append(row if prev is None else row + prev[1][k : k + 1, :])
    for a in range(own_n):
        at = slice(a * width, (a + 1) * width)
        outs[a][0:emb, :] = grad[:, at] * scale[:, at]
        for c in range(3):
            outs[a][emb + c : emb + c + 1, :] = -lines[c][:, at] * seen[:, at]
            outs[a][emb + 3 + c : emb + 4 + c, :] = lines[3 + c][:, at] * seen[:, at]
        outs[a][emb + 6 : emb + 8, :] = jnp.zeros((2, width), f32)
    loss = jnp.sum(lines[6] * own[6:7, :], axis=1, keepdims=True)
    outs[own_n][...] = jnp.broadcast_to(loss, outs[own_n].shape)


def pair_terms(own_blocks, col_blocks, prev, last, peers, weight_scale):
    own_n, col_n = len(own_blocks), len(col_blocks)
    emb, width = own_blocks[0].shape[0] - 8, own_blocks[0].shape[1]
    own_size, col_size = width * own_n, width * col_n
    chunk = 256 if col_size % 256 == 0 else 384 if col_size % 384 == 0 else 128
    strip = 256 if own_size % 256 == 0 else 128
    if last:
        out_shape = [jax.ShapeDtypeStruct((emb + 8, width), f32)] * own_n
        out_shape.append(jax.ShapeDtypeStruct((peers, 128), f32))
    else:
        out_shape = [
            jax.ShapeDtypeStruct((emb, own_size), f32),
            jax.ShapeDtypeStruct((8, own_size), f32),
        ]
    extra = [] if prev is None else list(prev)
    pairs = own_size * col_size
    return pl.pallas_call(
        functools.partial(
            pair_kernel, own_n, col_n, chunk, strip, 32, (prev is not None, last), weight_scale
        ),
        out_shape=out_shape,
        scratch_shapes=[
            pltpu.VMEM((3 * emb, own_size), bf16),
            pltpu.VMEM((col_size, 3 * emb), bf16),
            pltpu.VMEM((2 * emb, col_size), bf16),
            pltpu.VMEM((COMPS, col_size, 128), f32),
            pltpu.VMEM((chunk, own_size), f32),
            pltpu.VMEM((chunk, own_size), bf16),
            pltpu.VMEM((chunk, own_size), bf16),
            pltpu.VMEM((COMPS, 8, own_size), f32),
            pltpu.VMEM((8, own_size), f32),
            pltpu.VMEM((emb, own_size), f32),
        ],
        compiler_params=pltpu.CompilerParams(vmem_limit_bytes=40 * 2**20),
        cost_estimate=pl.CostEstimate(
            flops=pairs * 12 * emb, bytes_accessed=pairs * 4, transcendentals=3 * pairs
        ),
    )(*own_blocks, *col_blocks, *extra)


def pick(options, index):
    chosen = options[0]
    for n in range(1, len(options)):
        chosen = jnp.where(index == n, options[n], chosen)
    return chosen


def on_device(positions, embeddings, visible):
    frames_local, emb, width = embeddings.shape
    track_n, tm_n = lax.axis_size("track"), lax.axis_size("tm")
    tracks, frames = width * track_n, frames_local * tm_n
    weight_scale = rigidity / math.sqrt(tracks)
    team = 2 * frames_local
    teams = track_n // team

    def homes():
        for track in range(track_n):
            for tm in range(tm_n):
                yield track, tm

    def worker(track, tm, turn, shift):
        crew, member = divmod(track, team)
        frame = (turn + member) % frames_local
        core = tm % 2
        to_track = (crew + shift) % teams * team + core * frames_local + frame
        return to_track * tm_n + (tm - core + member // frames_local), frame

    def outward(turn, shift):
        return [(t * tm_n + m, worker(t, m, turn, shift)[0]) for t, m in homes()]

    def inward(turn):
        return [(worker(t, m, turn, 0)[0], t * tm_n + m) for t, m in homes()]

    def inward_next(turn):
        pairs = []
        for t, m in homes():
            at, frame = worker(t, m, turn, 0)
            if frame == frames_local - 1 and m + 1 < tm_n:
                pairs.append((at, t * tm_n + m + 1))
        return pairs

    swap = [(t * tm_n + m, t * tm_n + (m ^ 1)) for t, m in homes()]
    member = lax.rem(lax.axis_index("track"), team)
    turns = range(frames_local)

    seen = visible.astype(f32)
    rows = jnp.concatenate([positions, seen[None]], 0)
    following = lax.ppermute(rows[:, 0], "tm", [(i, i - 1) for i in range(1, tm_n)])
    rows = jnp.concatenate([rows, following[:, None]], 1)
    blocks = []
    for k in turns:
        blocks.append(
            jnp.concatenate(
                [
                    embeddings[k],
                    rows[:3, k],
                    rows[:3, k + 1],
                    rows[3:, k] * rows[3:, k + 1],
                    jnp.zeros((1, width), f32),
                ],
                0,
            )
        )
    sent = [pick(blocks, lax.rem(member + turn, frames_local)) for turn in turns]
    sent = lax.optimization_barrier(sent)
    arrived = [
        [lax.ppermute(sent[turn], AXES, outward(turn, shift)) for turn in turns]
        for shift in range(teams)
    ]

    def across(values):
        return [lax.ppermute(v, AXES, swap) for v in values]

    own = arrived[0]
    terms = functools.partial(pair_terms, own, peers=track_n * tm_n, weight_scale=weight_scale)
    beside = across(own)
    totals = terms(own, None, False)
    far = [v for shift in range(1, teams) for v in arrived[shift]]
    ready = beside
    for part in far[:-1]:
        part, totals = lax.optimization_barrier((part, totals))
        following = [part] + across([part])
        totals = terms(ready, totals, False)
        ready = following
    if far:
        totals = terms(ready, totals, False)
        part, totals = lax.optimization_barrier((far[-1], totals))
        ready = across([part])
        totals = terms([part], totals, False)
    totals = terms(ready, totals, True)

    back = [lax.ppermute(totals[turn], AXES, inward(turn)) for turn in turns]
    late = [lax.ppermute(totals[turn][emb:], AXES, inward_next(turn)) for turn in turns]
    shares = lax.all_to_all(totals[frames_local], AXES, 0, 0, tiled=True)
    total = jnp.sum(shares[:, :1]) * 0.25
    mean_loss = total / (tracks * (tracks - 1) / 2.0 * (frames - 1))

    of_frame = [
        pick(back, lax.rem(k - member + team * frames_local, frames_local)) for k in turns
    ]
    grad_emb = jnp.stack([v[:emb] for v in of_frame])
    from_before = sum(v[3:6] for v in late)
    grad_pos = []
    for k in turns:
        extra = from_before if k == 0 else of_frame[k - 1][emb + 3 : emb + 6]
        grad_pos.append(of_frame[k][emb : emb + 3] + extra)
    return (jnp.stack(grad_pos, 1), grad_emb, mean_loss)


def solution(mesh):
    in_specs = (P(None, "tm", "track"), P("tm", None, "track"), P("tm", "track"))
    out_specs = (P(None, "tm", "track"), P("tm", None, "track"), P())
    return jax.shard_map(
        on_device, mesh=mesh, in_specs=in_specs, out_specs=out_specs, check_vma=False
    )
```

```python
import functools
import math

import jax
import jax.numpy as jnp
from jax import lax
from jax.experimental import pallas as pl
from jax.experimental.pallas import tpu as pltpu
from jax.sharding import PartitionSpec as P

f32 = jnp.float32
bf16 = jnp.bfloat16
rigidity = 4.0
AXES = ("track", "tm")
TAIL = 8
GEO = 128
LEFT = (0, 0, 1, 0, 2, 1, 1, 2)
RIGHT = (0, 1, 0, 2, 0, 1, 2, 1)


def split(values):
    high = values.astype(bf16)
    return high, (values - high.astype(f32)).astype(bf16)


def split3(values):
    high = values.astype(bf16).astype(f32)
    rest = values - high
    mid = rest.astype(bf16).astype(f32)
    return high, mid, rest - mid


def geometry(ref, points, centre, left):
    size = points.shape[1]
    start = points[0:3] - centre[0:3]
    end = points[3:6] - centre[3:6]
    move = end - start
    square = jnp.sum(start * start, axis=0, keepdims=True)
    growth = jnp.sum(move * (start + end), axis=0, keepdims=True)
    ones = [jnp.ones((1, size), f32)] * 3
    if left:
        order, factor, factors = LEFT, -2.0, (start, start, move)
        tails = (list(split3(square)) + ones, list(split3(growth)) + ones)
    else:
        order, factor, factors = RIGHT, 1.0, (start, move, end)
        tails = (ones + list(split3(square + 1.0)), ones + list(split3(growth)))
    ref[...] = jnp.zeros_like(ref)
    parts = [split3(v) for v in factors]
    for at, group, tail in ((0, parts[:1], tails[0]), (32, parts[1:], tails[1])):
        for part in group:
            for k in order:
                ref[at : at + 3, :] = factor * part[k]
                at += 3
        for row in tail:
            ref[at : at + 1, :] = row
            at += 1
    return start, end


def pair_kernel(own_n, col_n, chunk, strip, rows, first, last, weight_scale, *refs):
    refs = list(refs)

    def take(count):
        taken = refs[:count]
        del refs[:count]
        return taken

    own_blocks, col_blocks = take(own_n), take(col_n)
    prev = take(0 if first else 2)
    kept = take(0 if first else 2)
    outs = take(own_n + 1 if last else 2)
    if first:
        kept = take(2)
    weights, geo_weights = kept
    lhs, geo_lhs, emb_split, pts_split, geo_own, geo_col, grad, sums, energies, own = take(10)
    logits, geo, g_high, g_low = take(2), take(2), take(2), take(2)
    pulls = [take(4), take(4)]
    emb, width = own_blocks[0].shape[0] - TAIL, own_blocks[0].shape[1]
    own_size, col_size = width * own_n, width * col_n
    inv_root = 1.0 / math.sqrt(emb)
    for a in range(own_n):
        own[:, a * width : (a + 1) * width] = own_blocks[a][emb : emb + TAIL, :]
    centre = jnp.mean(own[0:6, :], axis=1, keepdims=True)
    if first:
        for a in range(own_n):
            at = slice(a * width, (a + 1) * width)
            high, low = split(own_blocks[a][0:emb, :] * (0.5 * inv_root))
            weights[0:emb, at] = high
            weights[emb : 2 * emb, at] = low
            weights[2 * emb : 3 * emb, at] = high
        row = lax.broadcasted_iota(jnp.int32, (emb, own_size), 0)
        weights[3 * emb : 4 * emb, :] = jnp.where(row == 0, 1.0, 0.0).astype(bf16)
        geometry(geo_own, own[...], centre, True)
        row = lax.broadcasted_iota(jnp.int32, (GEO, own_size), 0)
        values = geo_own[...]
        geo_weights[:, 0:own_size] = jnp.where(row < 32, values, 0.0).astype(bf16)
        geo_weights[:, own_size : 2 * own_size] = jnp.where(row < 32, 0.0, values).astype(bf16)
    for b in range(col_n):
        at = slice(b * width, (b + 1) * width)
        values = col_blocks[b][0:emb, :]
        high, low = split(values)
        emb_split[0:emb, at] = high
        emb_split[emb : 2 * emb, at] = low
        high, low = split(values.T)
        lhs[at, 0:emb] = high
        lhs[at, emb : 2 * emb] = high
        lhs[at, 2 * emb : 3 * emb] = low
        points = col_blocks[b][emb : emb + TAIL, :]
        start, end = geometry(geo_col, points, centre, False)
        geo_col[96:97, :] = (points[6:7, :] - 1.0) * 1e4
        flipped = geo_col[...].T
        geo_lhs[at, :] = flipped.astype(bf16)
        hidden = jnp.broadcast_to(flipped[:, 96:97], (width, emb))
        column = lax.broadcasted_iota(jnp.int32, (width, emb), 1)
        lhs[at, 3 * emb : 4 * emb] = jnp.where(column == 0, hidden, 0.0).astype(bf16)
        ones, zeros = jnp.ones((1, width), f32), jnp.zeros((1, width), f32)
        centred = jnp.concatenate([start, end, ones, zeros], 0)
        for k, part in enumerate(split3(centred)):
            pts_split[8 * k : 8 * k + 8, at] = part.astype(bf16)
    if first:
        grad[...] = jnp.zeros_like(grad)
        sums[...] = jnp.zeros_like(sums)
        energies[...] = jnp.zeros_like(energies)
    else:
        grad[...] = prev[0][...]
        sums[...] = prev[1][0:16, :]
        energies[...] = prev[1][16:24, :]

    def products(n, i, k):
        cols, at = pl.ds(n * chunk, chunk), slice(i * strip, (i + 1) * strip)
        logits[k][...] = jnp.dot(lhs[cols, :], weights[:, at], preferred_element_type=f32)
        side = geo_lhs[cols, :]
        geo[k][0] = jnp.dot(side, geo_weights[:, at], preferred_element_type=f32)
        at = slice(own_size + i * strip, own_size + (i + 1) * strip)
        geo[k][1] = jnp.dot(side, geo_weights[:, at], preferred_element_type=f32)

    def elementwise(n, i, k):
        mine = slice(i * strip, (i + 1) * strip)
        total = energies[:, mine]
        for b in range(0, chunk, rows):
            at = slice(b, b + rows)
            sq0, growth = geo[k][0, at, :], geo[k][1, at, :]
            sq1 = sq0 + growth
            inv0, inv1 = lax.rsqrt(sq0), lax.rsqrt(sq1)
            both = sq1 * inv1 + sq0 * inv0
            change = growth * lax.rsqrt(both * both)
            tanh = jnp.tanh(logits[k][at, :])
            pull = change + change * tanh
            energy = pull * change
            g_high[k][at, :], g_low[k][at, :] = split(energy - energy * tanh)
            pulls[k][0][at, :], pulls[k][1][at, :] = split(pull * inv0)
            pulls[k][2][at, :], pulls[k][3][at, :] = split(pull * inv1)
            total = total + energy.reshape(rows // 8, 8, strip).sum(0)
        energies[:, mine] = total

    def gradients(n, i, k):
        cols, at = pl.ds(n * chunk, chunk), slice(i * strip, (i + 1) * strip)
        two = jnp.dot(emb_split[:, cols], g_high[k][...], preferred_element_type=f32)
        one = jnp.dot(emb_split[0:emb, cols], g_low[k][...], preferred_element_type=f32)
        grad[:, at] += two[:emb] + two[emb:] + one
        side = pts_split[:, cols]
        for frame in range(2):
            high, low = pulls[k][2 * frame], pulls[k][2 * frame + 1]
            moved = jnp.dot(side, high[...], preferred_element_type=f32)
            moved = moved + jnp.dot(side, low[...], preferred_element_type=f32)
            sums[8 * frame : 8 * frame + 8, at] += moved[:8] + moved[8:16] + moved[16:]

    tiles = [(n, i) for n in range(col_size // chunk) for i in range(own_size // strip)]
    products(*tiles[0], 0)
    for t, (n, i) in enumerate(tiles):
        if t + 1 < len(tiles):
            products(*tiles[t + 1], (t + 1) % 2)
        elementwise(n, i, t % 2)
        gradients(n, i, t % 2)

    if not last:
        outs[0][...] = grad[...]
        outs[1][0:16, :] = sums[...]
        outs[1][16:24, :] = energies[...]
        return
    seen = own[6:7, :] * weight_scale
    scale = seen * (0.25 * inv_root)
    start, end = own[0:3, :] - centre[0:3], own[3:6, :] - centre[3:6]
    from_start = (sums[0:3, :] - start * sums[6:7, :]) * seen
    from_end = (end * sums[14:15, :] - sums[11:14, :]) * seen
    for a in range(own_n):
        at = slice(a * width, (a + 1) * width)
        outs[a][0:emb, :] = grad[:, at] * scale[:, at]
        outs[a][emb : emb + 3, :] = from_start[:, at]
        outs[a][emb + 3 : emb + 6, :] = from_end[:, at]
        outs[a][emb + 6 : emb + 8, :] = jnp.zeros((2, width), f32)
    loss = jnp.sum(energies[...] * own[6:7, :], axis=0, keepdims=True)
    loss = jnp.sum(loss, axis=1, keepdims=True)
    outs[own_n][...] = jnp.broadcast_to(loss, outs[own_n].shape)


def pair_terms(own_blocks, col_blocks, prev, last, peers, weight_scale):
    own_n, col_n = len(own_blocks), len(col_blocks)
    emb, width = own_blocks[0].shape[0] - TAIL, own_blocks[0].shape[1]
    own_size, col_size = width * own_n, width * col_n
    chunk = 256 if col_size % 256 == 0 else 384 if col_size % 384 == 0 else 128
    strip = 256 if own_size % 256 == 0 else 128
    first = prev is None
    if last:
        out_shape = [jax.ShapeDtypeStruct((emb + TAIL, width), f32)] * own_n
        out_shape.append(jax.ShapeDtypeStruct((peers, 128), f32))
    else:
        out_shape = [
            jax.ShapeDtypeStruct((emb, own_size), f32),
            jax.ShapeDtypeStruct((24, own_size), f32),
        ]
    if first:
        out_shape.append(jax.ShapeDtypeStruct((4 * emb, own_size), bf16))
        out_shape.append(jax.ShapeDtypeStruct((GEO, 2 * own_size), bf16))
    pairs = own_size * col_size
    tile = (chunk, strip)
    made = pl.pallas_call(
        functools.partial(
            pair_kernel, own_n, col_n, chunk, strip, 32, first, last, weight_scale
        ),
        out_shape=out_shape,
        scratch_shapes=[
            pltpu.VMEM((col_size, 4 * emb), bf16),
            pltpu.VMEM((col_size, GEO), bf16),
            pltpu.VMEM((2 * emb, col_size), bf16),
            pltpu.VMEM((24, col_size), bf16),
            pltpu.VMEM((GEO, own_size), f32),
            pltpu.VMEM((GEO, width), f32),
            pltpu.VMEM((emb, own_size), f32),
            pltpu.VMEM((16, own_size), f32),
            pltpu.VMEM((8, own_size), f32),
            pltpu.VMEM((8, own_size), f32),
        ]
        + [pltpu.VMEM(tile, f32)] * 2
        + [pltpu.VMEM((2, *tile), f32)] * 2
        + [pltpu.VMEM(tile, bf16)] * 12,
        compiler_params=pltpu.CompilerParams(vmem_limit_bytes=32 * 2**20),
        cost_estimate=pl.CostEstimate(
            flops=pairs * 12 * emb, bytes_accessed=pairs * 4, transcendentals=3 * pairs
        ),
    )(*own_blocks, *col_blocks, *(() if first else prev))
    return made if last else made[:2] + (made[2:] if first else prev[2:])


def pick(options, index):
    chosen = options[0]
    for n in range(1, len(options)):
        chosen = jnp.where(index == n, options[n], chosen)
    return chosen


def on_device(positions, embeddings, visible):
    frames_local, emb, width = embeddings.shape
    track_n, tm_n = lax.axis_size("track"), lax.axis_size("tm")
    tracks, frames = width * track_n, frames_local * tm_n
    weight_scale = rigidity / math.sqrt(tracks)
    team = 2 * frames_local
    teams = track_n // team

    def homes():
        for track in range(track_n):
            for tm in range(tm_n):
                yield track, tm

    def worker(track, tm, turn, shift):
        crew, member = divmod(track, team)
        frame = (turn + member) % frames_local
        core = tm % 2
        to_track = (crew + shift) % teams * team + core * frames_local + frame
        return to_track * tm_n + (tm - core + member // frames_local), frame

    def outward(turn, shift):
        return [(t * tm_n + m, worker(t, m, turn, shift)[0]) for t, m in homes()]

    def inward(turn):
        return [(worker(t, m, turn, 0)[0], t * tm_n + m) for t, m in homes()]

    def inward_next(turn):
        pairs = []
        for t, m in homes():
            at, frame = worker(t, m, turn, 0)
            if frame == frames_local - 1 and m + 1 < tm_n:
                pairs.append((at, t * tm_n + m + 1))
        return pairs

    swap = [(t * tm_n + m, t * tm_n + (m ^ 1)) for t, m in homes()]
    member = lax.rem(lax.axis_index("track"), team)
    turns = range(frames_local)

    seen = visible.astype(f32)
    rows = jnp.concatenate([positions, seen[None]], 0)
    following = lax.ppermute(rows[:, 0], "tm", [(i, i - 1) for i in range(1, tm_n)])
    rows = jnp.concatenate([rows, following[:, None]], 1)
    blocks = []
    for k in turns:
        blocks.append(
            jnp.concatenate(
                [
                    embeddings[k],
                    rows[:3, k],
                    rows[:3, k + 1],
                    rows[3:, k] * rows[3:, k + 1],
                    jnp.zeros((1, width), f32),
                ],
                0,
            )
        )
    sent = [pick(blocks, lax.rem(member + turn, frames_local)) for turn in turns]
    sent = lax.optimization_barrier(sent)
    arrived = [
        [lax.ppermute(sent[turn], AXES, outward(turn, shift)) for turn in turns]
        for shift in range(teams)
    ]

    def across(values):
        return [lax.ppermute(v, AXES, swap) for v in values]

    own = arrived[0]
    terms = functools.partial(pair_terms, own, peers=track_n * tm_n, weight_scale=weight_scale)
    beside = across(own)
    totals = terms(own, None, False)
    far = [v for shift in range(1, teams) for v in arrived[shift]]
    ready = beside
    for part in far[:-1]:
        part, totals = lax.optimization_barrier((part, totals))
        following = [part] + across([part])
        totals = terms(ready, totals, False)
        ready = following
    if far:
        totals = terms(ready, totals, False)
        part, totals = lax.optimization_barrier((far[-1], totals))
        ready = across([part])
        totals = terms([part], totals, False)
    totals = terms(ready, totals, True)

    back = [lax.ppermute(totals[turn], AXES, inward(turn)) for turn in turns]
    late = [lax.ppermute(totals[turn][emb:], AXES, inward_next(turn)) for turn in turns]
    shares = lax.all_to_all(totals[frames_local], AXES, 0, 0, tiled=True)
    total = jnp.sum(shares[:, :1]) * 0.25
    mean_loss = total / (tracks * (tracks - 1) / 2.0 * (frames - 1))

    of_frame = [
        pick(back, lax.rem(k - member + team * frames_local, frames_local)) for k in turns
    ]
    grad_emb = jnp.stack([v[:emb] for v in of_frame])
    from_before = sum(v[3:6] for v in late)
    grad_pos = []
    for k in turns:
        extra = from_before if k == 0 else of_frame[k - 1][emb + 3 : emb + 6]
        grad_pos.append(of_frame[k][emb : emb + 3] + extra)
    return (jnp.stack(grad_pos, 1), grad_emb, mean_loss)


def solution(mesh):
    in_specs = (P(None, "tm", "track"), P("tm", None, "track"), P("tm", "track"))
    out_specs = (P(None, "tm", "track"), P("tm", None, "track"), P())
    return jax.shard_map(
        on_device, mesh=mesh, in_specs=in_specs, out_specs=out_specs, check_vma=False
    )
```

```python
import functools
import math

import jax
import jax.numpy as jnp
from jax import lax
from jax.experimental import pallas as pl
from jax.experimental.pallas import tpu as pltpu
from jax.sharding import PartitionSpec as P

f32 = jnp.float32
bf16 = jnp.bfloat16
rigidity = 4.0
AXES = ("track", "tm")
TAIL = 8
GEO = 128
LEFT = (0, 0, 1, 0, 2, 1, 1, 2)
RIGHT = (0, 1, 0, 2, 0, 1, 2, 1)


def split(values):
    high = values.astype(bf16)
    return high, (values - high.astype(f32)).astype(bf16)


def split3(values):
    high = values.astype(bf16).astype(f32)
    rest = values - high
    mid = rest.astype(bf16).astype(f32)
    return high, mid, rest - mid


def geometry(ref, points, centre, left):
    size = points.shape[1]
    start = points[0:3] - centre[0:3]
    end = points[3:6] - centre[3:6]
    move = end - start
    square = jnp.sum(start * start, axis=0, keepdims=True)
    growth = jnp.sum(move * (start + end), axis=0, keepdims=True)
    ones = [jnp.ones((1, size), f32)] * 3
    if left:
        order, factor, factors = LEFT, -2.0, (start, start, move)
        tails = (list(split3(square)) + ones, list(split3(growth)) + ones)
    else:
        order, factor, factors = RIGHT, 1.0, (start, move, end)
        tails = (ones + list(split3(square + 1.0)), ones + list(split3(growth)))
    ref[...] = jnp.zeros_like(ref)
    parts = [split3(v) for v in factors]
    for at, group, tail in ((0, parts[:1], tails[0]), (32, parts[1:], tails[1])):
        for part in group:
            for k in order:
                ref[at : at + 3, :] = factor * part[k]
                at += 3
        for row in tail:
            ref[at : at + 1, :] = row
            at += 1
    return start, end


def pair_kernel(own_n, col_n, chunk, rows, first, home, lanes, energy, weight_scale, *refs):
    refs = list(refs)

    def take(count):
        taken = refs[:count]
        del refs[:count]
        return taken

    own_blocks, col_blocks = take(own_n), take(col_n)
    prev = take(0 if first else 2)
    kept = take(0 if first else 2)
    outs = take(2 if home is None else len(home) + (energy is not None))
    if first:
        kept = take(2)
    weights, geo_weights = kept
    lhs, geo_lhs, emb_split, pts_split, geo_own, geo_col, grad, sums, energies, own = take(10)
    logits, geo, g_high, g_low = take(2), take(2), take(2), take(2)
    pulls = [take(4), take(4)]
    emb, width = own_blocks[0].shape[0] - TAIL, own_blocks[0].shape[1]
    own_size, col_size = width * own_n, width * col_n
    inv_root = 1.0 / math.sqrt(emb)
    for a in range(own_n):
        own[:, a * width : (a + 1) * width] = own_blocks[a][emb : emb + TAIL, :]
    centre = jnp.mean(own[0:6, :], axis=1, keepdims=True)
    if first:
        for a in range(own_n):
            at = slice(a * width, (a + 1) * width)
            high, low = split(own_blocks[a][0:emb, :] * (0.5 * inv_root))
            weights[0:emb, at] = high
            weights[emb : 2 * emb, at] = low
            weights[2 * emb : 3 * emb, at] = high
        row = lax.broadcasted_iota(jnp.int32, (emb, own_size), 0)
        weights[3 * emb : 4 * emb, :] = jnp.where(row == 0, 1.0, 0.0).astype(bf16)
        geometry(geo_own, own[...], centre, True)
        row = lax.broadcasted_iota(jnp.int32, (GEO, own_size), 0)
        values = geo_own[...]
        geo_weights[:, 0:own_size] = jnp.where(row < 32, values, 0.0).astype(bf16)
        geo_weights[:, own_size : 2 * own_size] = jnp.where(row < 32, 0.0, values).astype(bf16)
    for b in range(col_n):
        at = slice(b * width, (b + 1) * width)
        values = col_blocks[b][0:emb, :]
        high, low = split(values)
        emb_split[0:emb, at] = high
        emb_split[emb : 2 * emb, at] = low
        high, low = split(values.T)
        lhs[at, 0:emb] = high
        lhs[at, emb : 2 * emb] = high
        lhs[at, 2 * emb : 3 * emb] = low
        points = col_blocks[b][emb : emb + TAIL, :]
        start, end = geometry(geo_col, points, centre, False)
        geo_col[96:97, :] = (points[6:7, :] - 1.0) * 1e4
        flipped = geo_col[...].T
        geo_lhs[at, :] = flipped.astype(bf16)
        hidden = jnp.broadcast_to(flipped[:, 96:97], (width, emb))
        column = lax.broadcasted_iota(jnp.int32, (width, emb), 1)
        lhs[at, 3 * emb : 4 * emb] = jnp.where(column == 0, hidden, 0.0).astype(bf16)
        ones, zeros = jnp.ones((1, width), f32), jnp.zeros((1, width), f32)
        centred = jnp.concatenate([start, end, ones, zeros], 0)
        for k, part in enumerate(split3(centred)):
            pts_split[8 * k : 8 * k + 8, at] = part.astype(bf16)
    if first:
        grad[...] = jnp.zeros_like(grad)
        sums[...] = jnp.zeros_like(sums)
        energies[...] = jnp.zeros_like(energies)
    else:
        grad[...] = prev[0][...]
        sums[...] = prev[1][0:16, :]
        energies[...] = prev[1][16:24, :]

    def products(n, i, k):
        cols, at = pl.ds(n * chunk, chunk), slice(*i)
        size = i[1] - i[0]
        logits[k][:, :size] = jnp.dot(lhs[cols, :], weights[:, at], preferred_element_type=f32)
        side = geo_lhs[cols, :]
        geo[k][0, :, :size] = jnp.dot(side, geo_weights[:, at], preferred_element_type=f32)
        at = slice(own_size + i[0], own_size + i[1])
        geo[k][1, :, :size] = jnp.dot(side, geo_weights[:, at], preferred_element_type=f32)

    def elementwise(n, i, k):
        mine, size = slice(*i), i[1] - i[0]
        total = jnp.zeros((8, size), f32)
        for b in range(0, chunk, rows):
            at = slice(b, b + rows)
            sq0, growth = geo[k][0, at, :size], geo[k][1, at, :size]
            sq1 = sq0 + growth
            inv0, inv1 = lax.rsqrt(sq0), lax.rsqrt(sq1)
            both = sq1 * inv1 + sq0 * inv0
            change = growth * lax.rsqrt(both * both)
            tanh = jnp.tanh(logits[k][at, :size])
            pull = change + change * tanh
            value = pull * change
            g_high[k][at, :size], g_low[k][at, :size] = split(value - value * tanh)
            pulls[k][0][at, :size], pulls[k][1][at, :size] = split(pull * inv0)
            pulls[k][2][at, :size], pulls[k][3][at, :size] = split(pull * inv1)
            total = total + value.reshape(rows // 8, 8, size).sum(0)
        if energy is not None:
            column = lax.broadcasted_iota(jnp.int32, (8, size), 1) + i[0]
            factor = jnp.where(column >= energy, 2.0, 1.0) if energy < i[1] else 1.0
            energies[:, mine] += total * factor

    def gradients(n, i, k):
        cols, at, size = pl.ds(n * chunk, chunk), slice(*i), i[1] - i[0]
        two = jnp.dot(emb_split[:, cols], g_high[k][:, :size], preferred_element_type=f32)
        one = jnp.dot(emb_split[0:emb, cols], g_low[k][:, :size], preferred_element_type=f32)
        grad[:, at] += two[:emb] + two[emb:] + one
        side = pts_split[:, cols]
        for frame in range(2):
            high, low = pulls[k][2 * frame], pulls[k][2 * frame + 1]
            moved = jnp.dot(side, high[:, :size], preferred_element_type=f32)
            moved = moved + jnp.dot(side, low[:, :size], preferred_element_type=f32)
            sums[8 * frame : 8 * frame + 8, at] += moved[:8] + moved[8:16] + moved[16:]

    tiles = [(n, i) for n in range(col_size // chunk) for i in lanes]
    products(*tiles[0], 0)
    for t, (n, i) in enumerate(tiles):
        if t + 1 < len(tiles):
            products(*tiles[t + 1], (t + 1) % 2)
        elementwise(n, i, t % 2)
        gradients(n, i, t % 2)

    if home is None:
        outs[0][...] = grad[...]
        outs[1][0:16, :] = sums[...]
        outs[1][16:24, :] = energies[...]
        return
    for a, out in zip(home, outs):
        at = slice(a * width, (a + 1) * width)
        seen = own[6:7, at] * weight_scale
        start, end = own[0:3, at] - centre[0:3], own[3:6, at] - centre[3:6]
        out[0:emb, :] = grad[:, at] * (seen * (0.25 * inv_root))
        out[emb : emb + 3, :] = (sums[0:3, at] - start * sums[6:7, at]) * seen
        out[emb + 3 : emb + 6, :] = (end * sums[14:15, at] - sums[11:14, at]) * seen
        out[emb + 6 : emb + 8, :] = jnp.zeros((2, width), f32)
    if energy is not None:
        loss = jnp.sum(energies[...] * own[6:7, :], axis=0, keepdims=True)
        loss = jnp.sum(loss, axis=1, keepdims=True)
        outs[len(home)][...] = jnp.broadcast_to(loss, outs[len(home)].shape)


def pair_terms(
    own_blocks, col_blocks, prev, weight_scale, peers, home=None, double=None, counted=True
):
    own_n, col_n = len(own_blocks), len(col_blocks)
    emb, width = own_blocks[0].shape[0] - TAIL, own_blocks[0].shape[1]
    own_size, col_size = width * own_n, width * col_n
    chunk = 256 if col_size % 256 == 0 else 384 if col_size % 384 == 0 else 128
    low, high = (0, own_size) if home is None else (home[0] * width, (home[-1] + 1) * width)
    strip = 256 if (high - low) % 256 == 0 else 384 if (high - low) % 384 == 0 else 128
    lanes = [(i, i + strip) for i in range(low, high, strip)]
    energy = None
    if counted:
        energy = own_size if double is None else double * width
    first = prev is None
    if home is None:
        out_shape = [
            jax.ShapeDtypeStruct((emb, own_size), f32),
            jax.ShapeDtypeStruct((24, own_size), f32),
        ]
    else:
        out_shape = [jax.ShapeDtypeStruct((emb + TAIL, width), f32)] * len(home)
        if counted:
            out_shape.append(jax.ShapeDtypeStruct((peers, 128), f32))
    if first:
        out_shape.append(jax.ShapeDtypeStruct((4 * emb, own_size), bf16))
        out_shape.append(jax.ShapeDtypeStruct((GEO, 2 * own_size), bf16))
    pairs = (high - low) * col_size
    tile = (chunk, strip)
    return pl.pallas_call(
        functools.partial(
            pair_kernel, own_n, col_n, chunk, 32, first, home, lanes, energy, weight_scale
        ),
        out_shape=out_shape,
        scratch_shapes=[
            pltpu.VMEM((col_size, 4 * emb), bf16),
            pltpu.VMEM((col_size, GEO), bf16),
            pltpu.VMEM((2 * emb, col_size), bf16),
            pltpu.VMEM((24, col_size), bf16),
            pltpu.VMEM((GEO, own_size), f32),
            pltpu.VMEM((GEO, width), f32),
            pltpu.VMEM((emb, own_size), f32),
            pltpu.VMEM((16, own_size), f32),
            pltpu.VMEM((8, own_size), f32),
            pltpu.VMEM((8, own_size), f32),
        ]
        + [pltpu.VMEM(tile, f32)] * 2
        + [pltpu.VMEM((2, *tile), f32)] * 2
        + [pltpu.VMEM(tile, bf16)] * 12,
        compiler_params=pltpu.CompilerParams(vmem_limit_bytes=32 * 2**20),
        cost_estimate=pl.CostEstimate(
            flops=pairs * emb * 100, bytes_accessed=1, transcendentals=0
        ),
    )(*own_blocks, *col_blocks, *(() if first else prev))


def pick(options, index):
    chosen = options[0]
    for n in range(1, len(options)):
        chosen = jnp.where(index == n, options[n], chosen)
    return chosen


def on_device(positions, embeddings, visible):
    frames_local, emb, width = embeddings.shape
    track_n, tm_n = lax.axis_size("track"), lax.axis_size("tm")
    tracks, frames = width * track_n, frames_local * tm_n
    weight_scale = rigidity / math.sqrt(tracks)
    team = 2 * frames_local
    teams = track_n // team

    def homes():
        for track in range(track_n):
            for tm in range(tm_n):
                yield track, tm

    def worker(track, tm, turn, shift):
        crew, member = divmod(track, team)
        core = tm % 2
        frame = (turn + member) % frames_local
        to_track = (crew + shift) % teams * team + core * frames_local + frame
        return to_track * tm_n + (tm - core + member // frames_local), frame

    def outward(turn, shift):
        return [(t * tm_n + m, worker(t, m, turn, shift)[0]) for t, m in homes()]

    def inward(turn):
        return [(worker(t, m, turn, 0)[0], t * tm_n + m) for t, m in homes()]

    def inward_next(turn):
        pairs = []
        for t, m in homes():
            at, frame = worker(t, m, turn, 0)
            if frame == frames_local - 1 and m + 1 < tm_n:
                pairs.append((at, t * tm_n + m + 1))
        return pairs

    swap = [(t * tm_n + m, t * tm_n + (m ^ 1)) for t, m in homes()]
    member = lax.rem(lax.axis_index("track"), team)
    turns = range(frames_local)

    seen = visible.astype(f32)
    rows = jnp.concatenate([positions, seen[None]], 0)
    following = lax.ppermute(rows[:, 0], "tm", [(i, i - 1) for i in range(1, tm_n)])
    rows = jnp.concatenate([rows, following[:, None]], 1)
    blocks = []
    for k in turns:
        blocks.append(
            jnp.concatenate(
                [
                    embeddings[k],
                    rows[:3, k],
                    rows[:3, k + 1],
                    rows[3:, k] * rows[3:, k + 1],
                    jnp.zeros((1, width), f32),
                ],
                0,
            )
        )
    sent = [pick(blocks, lax.rem(member + turn, frames_local)) for turn in turns]
    sent = lax.optimization_barrier(sent)
    arrived = [
        [lax.ppermute(sent[turn], AXES, outward(turn, shift)) for turn in turns]
        for shift in range(teams)
    ]

    def across(values):
        return [lax.ppermute(v, AXES, swap) for v in values]

    own, far = arrived[0], [v for shift in range(1, teams) for v in arrived[shift]]
    terms = functools.partial(pair_terms, own, weight_scale=weight_scale, peers=track_n * tm_n)
    ready = across(own)
    made = terms(own, None)
    totals, kept = made[:2], made[2:]
    LOOK = 1
    for n in range(len(far)):
        ahead = far[n : n + LOOK]
        ahead, totals = lax.optimization_barrier((ahead, totals))
        far[n : n + LOOK] = ahead
        following = [far[n]] + across([far[n]])
        totals = terms(ready, [*totals, *kept])
        ready = following
    *done, loss = terms(ready, [*totals, *kept], home=list(turns))
    back = [lax.ppermute(done[turn], AXES, inward(turn)) for turn in turns]
    late = [lax.ppermute(done[turn][emb - 0:], AXES, inward_next(turn))[0:] for turn in turns]
    shares = lax.all_to_all(loss, AXES, 0, 0, tiled=True)
    of_frame = [
        pick(back, lax.rem(k - member + 2 * team * frames_local, frames_local)) for k in turns
    ]
    grad_emb = jnp.stack([v[:emb] for v in of_frame])
    before, grad_pos = sum(v[3:6] for v in late), jnp.zeros((3, frames_local, width), f32)
    frame = lax.broadcasted_iota(jnp.int32, grad_pos.shape, 1)
    for k, v in enumerate(of_frame):
        moved = v[emb : emb + 3] + before
        before = v[emb + 3 : emb + 6]
        grad_pos = jnp.where(frame == k, moved[:, None, :], grad_pos)
    shares, grad_emb = lax.optimization_barrier((shares, grad_emb))
    mean_loss = jnp.sum(shares[:, :1]) * 0.25 / (tracks * (tracks - 1) / 2.0 * (frames - 1))
    return (grad_pos, grad_emb, mean_loss)


def solution(mesh):
    in_specs = (P(None, "tm", "track"), P("tm", None, "track"), P("tm", "track"))
    out_specs = (P(None, "tm", "track"), P("tm", None, "track"), P())
    return jax.shard_map(
        on_device, mesh=mesh, in_specs=in_specs, out_specs=out_specs, check_vma=False
    )
```

```python
import functools
import math

import jax
import jax.numpy as jnp
from jax import lax
from jax.experimental import pallas as pl
from jax.experimental.pallas import tpu as pltpu
from jax.sharding import PartitionSpec as P

f32 = jnp.float32
bf16 = jnp.bfloat16
rigidity = 4.0
AXES = ("track", "tm")
TAIL = 8
GEO = 128
LEFT = (0, 0, 1, 0, 2, 1, 1, 2)
RIGHT = (0, 1, 0, 2, 0, 1, 2, 1)


def split(values):
    high = values.astype(bf16)
    return high, (values - high.astype(f32)).astype(bf16)


def split3(values):
    high = values.astype(bf16).astype(f32)
    rest = values - high
    mid = rest.astype(bf16).astype(f32)
    return high, mid, rest - mid


def geometry(ref, points, centre, left):
    size = points.shape[1]
    start = points[0:3] - centre[0:3]
    end = points[3:6] - centre[3:6]
    move = end - start
    square = jnp.sum(start * start, axis=0, keepdims=True)
    growth = jnp.sum(move * (start + end), axis=0, keepdims=True)
    ones = [jnp.ones((1, size), f32)] * 3
    if left:
        order, factor, factors = LEFT, -2.0, (start, start, move)
        tails = (list(split3(square)) + ones, list(split3(growth)) + ones)
    else:
        order, factor, factors = RIGHT, 1.0, (start, move, end)
        tails = (ones + list(split3(square + 1.0)), ones + list(split3(growth)))
    ref[...] = jnp.zeros_like(ref)
    parts = [split3(v) for v in factors]
    for at, group, tail in ((0, parts[:1], tails[0]), (32, parts[1:], tails[1])):
        for part in group:
            for k in order:
                ref[at : at + 3, :] = factor * part[k]
                at += 3
        for row in tail:
            ref[at : at + 1, :] = row
            at += 1
    return start, end


def pair_kernel(own_n, col_n, chunk, rows, first, home, lanes, energy, weight_scale, *refs):
    refs = list(refs)

    def take(count):
        taken = refs[:count]
        del refs[:count]
        return taken

    own_blocks, col_blocks = take(own_n), take(col_n)
    prev = take(0 if first else 2)
    kept = take(0 if first else 2)
    outs = take(2 if home is None else len(home) + (energy is not None))
    if first:
        kept = take(2)
    weights, geo_weights = kept
    lhs, geo_lhs, emb_split, pts_split, geo_own, geo_col, grad, sums, energies, own = take(10)
    logits, geo, g_high, g_low = take(2), take(2), take(2), take(2)
    pulls = [take(4), take(4)]
    emb, width = own_blocks[0].shape[0] - TAIL, own_blocks[0].shape[1]
    own_size, col_size = width * own_n, width * col_n
    inv_root = 1.0 / math.sqrt(emb)
    for a in range(own_n):
        own[:, a * width : (a + 1) * width] = own_blocks[a][emb : emb + TAIL, :]
    centre = jnp.mean(own[0:6, :], axis=1, keepdims=True)
    if first:
        for a in range(own_n):
            at = slice(a * width, (a + 1) * width)
            high, low = split(own_blocks[a][0:emb, :] * (0.5 * inv_root))
            weights[0:emb, at] = high
            weights[emb : 2 * emb, at] = low
            weights[2 * emb : 3 * emb, at] = high
        geometry(geo_own, own[...], centre, True)
        row = lax.broadcasted_iota(jnp.int32, (GEO, own_size), 0)
        values = geo_own[...]
        geo_weights[:, 0:own_size] = jnp.where(row < 32, values, 0.0).astype(bf16)
        geo_weights[:, own_size : 2 * own_size] = jnp.where(row < 32, 0.0, values).astype(bf16)
    for b in range(col_n):
        at = slice(b * width, (b + 1) * width)
        values = col_blocks[b][0:emb, :]
        high, low = split(values)
        emb_split[0:emb, at] = high
        emb_split[emb : 2 * emb, at] = low
        high, low = split(values.T)
        lhs[at, 0:emb] = high
        lhs[at, emb : 2 * emb] = high
        lhs[at, 2 * emb : 3 * emb] = low
        points = col_blocks[b][emb : emb + TAIL, :]
        start, end = geometry(geo_col, points, centre, False)
        geo_col[32:96, :] = geo_col[32:96, :] * points[6:7, :]
        geo_lhs[at, :] = geo_col[...].T.astype(bf16)
        ones, zeros = jnp.ones((1, width), f32), jnp.zeros((1, width), f32)
        centred = jnp.concatenate([start, end, ones, zeros], 0)
        for k, part in enumerate(split3(centred)):
            pts_split[8 * k : 8 * k + 8, at] = part.astype(bf16)
    if first:
        grad[...] = jnp.zeros_like(grad)
        sums[...] = jnp.zeros_like(sums)
        energies[...] = jnp.zeros_like(energies)
    else:
        grad[...] = prev[0][...]
        sums[...] = prev[1][0:16, :]
        energies[...] = prev[1][16:24, :]

    def products(n, i, k):
        cols, at = pl.ds(n * chunk, chunk), slice(*i)
        size = i[1] - i[0]
        logits[k][:, :size] = jnp.dot(lhs[cols, :], weights[:, at], preferred_element_type=f32)
        side = geo_lhs[cols, :]
        geo[k][0, :, :size] = jnp.dot(side, geo_weights[:, at], preferred_element_type=f32)
        at = slice(own_size + i[0], own_size + i[1])
        geo[k][1, :, :size] = jnp.dot(side, geo_weights[:, at], preferred_element_type=f32)

    def elementwise(n, i, k):
        mine, size = slice(*i), i[1] - i[0]
        total = jnp.zeros((8, size), f32)
        for b in range(0, chunk, rows):
            at = slice(b, b + rows)
            sq0, growth = geo[k][0, at, :size], geo[k][1, at, :size]
            sq1 = sq0 + growth
            inv0, inv1 = lax.rsqrt(sq0), lax.rsqrt(sq1)
            both = sq1 * inv1 + sq0 * inv0
            change = growth * lax.rsqrt(both * both)
            tanh = jnp.tanh(logits[k][at, :size])
            pull = change + change * tanh
            value = pull * change
            g_high[k][at, :size], g_low[k][at, :size] = split(value - value * tanh)
            pulls[k][0][at, :size], pulls[k][1][at, :size] = split(pull * inv0)
            pulls[k][2][at, :size], pulls[k][3][at, :size] = split(pull * inv1)
            total = total + value.reshape(rows // 8, 8, size).sum(0)
        if energy is not None:
            column = lax.broadcasted_iota(jnp.int32, (8, size), 1) + i[0]
            factor = jnp.where(column >= energy, 2.0, 1.0) if energy < i[1] else 1.0
            energies[:, mine] += total * factor

    def gradients(n, i, k):
        cols, at, size = pl.ds(n * chunk, chunk), slice(*i), i[1] - i[0]
        two = jnp.dot(emb_split[:, cols], g_high[k][:, :size], preferred_element_type=f32)
        one = jnp.dot(emb_split[0:emb, cols], g_low[k][:, :size], preferred_element_type=f32)
        grad[:, at] += two[:emb] + two[emb:] + one
        side = pts_split[:, cols]
        for frame in range(2):
            high, low = pulls[k][2 * frame], pulls[k][2 * frame + 1]
            moved = jnp.dot(side, high[:, :size], preferred_element_type=f32)
            moved = moved + jnp.dot(side, low[:, :size], preferred_element_type=f32)
            sums[8 * frame : 8 * frame + 8, at] += moved[:8] + moved[8:16] + moved[16:]

    tiles = [(n, i) for n in range(col_size // chunk) for i in lanes]
    products(*tiles[0], 0)
    for t, (n, i) in enumerate(tiles):
        if t + 1 < len(tiles):
            products(*tiles[t + 1], (t + 1) % 2)
        elementwise(n, i, t % 2)
        gradients(n, i, t % 2)

    if home is None:
        outs[0][...] = grad[...]
        outs[1][0:16, :] = sums[...]
        outs[1][16:24, :] = energies[...]
        return
    for a, out in zip(home, outs):
        at = slice(a * width, (a + 1) * width)
        seen = own[6:7, at] * weight_scale
        start, end = own[0:3, at] - centre[0:3], own[3:6, at] - centre[3:6]
        out[0:emb, :] = grad[:, at] * (seen * (0.25 * inv_root))
        out[emb : emb + 3, :] = (sums[0:3, at] - start * sums[6:7, at]) * seen
        out[emb + 3 : emb + 6, :] = (end * sums[14:15, at] - sums[11:14, at]) * seen
        out[emb + 6 : emb + 8, :] = jnp.zeros((2, width), f32)
    if energy is not None:
        loss = jnp.sum(energies[...] * own[6:7, :], axis=0, keepdims=True)
        loss = jnp.sum(loss, axis=1, keepdims=True)
        outs[len(home)][...] = jnp.broadcast_to(loss, outs[len(home)].shape)


def pair_terms(
    own_blocks, col_blocks, prev, weight_scale, peers, home=None, double=None, counted=True
):
    own_n, col_n = len(own_blocks), len(col_blocks)
    emb, width = own_blocks[0].shape[0] - TAIL, own_blocks[0].shape[1]
    own_size, col_size = width * own_n, width * col_n
    chunk = 256 if col_size % 256 == 0 else 384 if col_size % 384 == 0 else 128
    low, high = (0, own_size) if home is None else (home[0] * width, (home[-1] + 1) * width)
    strip = 256 if (high - low) % 256 == 0 else 384 if (high - low) % 384 == 0 else 128
    lanes = [(i, i + strip) for i in range(low, high, strip)]
    energy = None
    if counted:
        energy = own_size if double is None else double * width
    first = prev is None
    if home is None:
        out_shape = [
            jax.ShapeDtypeStruct((emb, own_size), f32),
            jax.ShapeDtypeStruct((24, own_size), f32),
        ]
    else:
        out_shape = [jax.ShapeDtypeStruct((emb + TAIL, width), f32)] * len(home)
        if counted:
            out_shape.append(jax.ShapeDtypeStruct((peers, 128), f32))
    if first:
        out_shape.append(jax.ShapeDtypeStruct((3 * emb, own_size), bf16))
        out_shape.append(jax.ShapeDtypeStruct((GEO, 2 * own_size), bf16))
    pairs = (high - low) * col_size
    tile = (chunk, strip)
    return pl.pallas_call(
        functools.partial(
            pair_kernel, own_n, col_n, chunk, 32, first, home, lanes, energy, weight_scale
        ),
        out_shape=out_shape,
        scratch_shapes=[
            pltpu.VMEM((col_size, 3 * emb), bf16),
            pltpu.VMEM((col_size, GEO), bf16),
            pltpu.VMEM((2 * emb, col_size), bf16),
            pltpu.VMEM((24, col_size), bf16),
            pltpu.VMEM((GEO, own_size), f32),
            pltpu.VMEM((GEO, width), f32),
            pltpu.VMEM((emb, own_size), f32),
            pltpu.VMEM((16, own_size), f32),
            pltpu.VMEM((8, own_size), f32),
            pltpu.VMEM((8, own_size), f32),
        ]
        + [pltpu.VMEM(tile, f32)] * 2
        + [pltpu.VMEM((2, *tile), f32)] * 2
        + [pltpu.VMEM(tile, bf16)] * 12,
        compiler_params=pltpu.CompilerParams(vmem_limit_bytes=32 * 2**20),
        cost_estimate=pl.CostEstimate(
            flops=pairs * emb * 100, bytes_accessed=1, transcendentals=0
        ),
    )(*own_blocks, *col_blocks, *(() if first else prev))


def pick(options, index):
    chosen = options[0]
    for n in range(1, len(options)):
        chosen = jnp.where(index == n, options[n], chosen)
    return chosen


def on_device(positions, embeddings, visible):
    frames_local, emb, width = embeddings.shape
    track_n, tm_n = lax.axis_size("track"), lax.axis_size("tm")
    tracks, frames = width * track_n, frames_local * tm_n
    weight_scale = rigidity / math.sqrt(tracks)
    team = 2 * frames_local
    teams = track_n // team

    def homes():
        for track in range(track_n):
            for tm in range(tm_n):
                yield track, tm

    def worker(track, tm, turn, shift):
        crew, member = divmod(track, team)
        core = tm % 2
        frame = (turn + member) % frames_local
        to_track = (crew + shift) % teams * team + core * frames_local + frame
        return to_track * tm_n + (tm - core + member // frames_local), frame

    def outward(turn, shift):
        return [(t * tm_n + m, worker(t, m, turn, shift)[0]) for t, m in homes()]

    def inward(turn):
        return [(worker(t, m, turn, 0)[0], t * tm_n + m) for t, m in homes()]

    def inward_next(turn):
        pairs = []
        for t, m in homes():
            at, frame = worker(t, m, turn, 0)
            if frame == frames_local - 1 and m + 1 < tm_n:
                pairs.append((at, t * tm_n + m + 1))
        return pairs

    swap = [(t * tm_n + m, t * tm_n + (m ^ 1)) for t, m in homes()]
    member = lax.rem(lax.axis_index("track"), team)
    turns = range(frames_local)

    seen = visible.astype(f32)
    rows = jnp.concatenate([positions, seen[None]], 0)
    following = lax.ppermute(rows[:, 0], "tm", [(i, i - 1) for i in range(1, tm_n)])
    rows = jnp.concatenate([rows, following[:, None]], 1)
    blocks = []
    for k in turns:
        blocks.append(
            jnp.concatenate(
                [
                    embeddings[k],
                    rows[:3, k],
                    rows[:3, k + 1],
                    rows[3:, k] * rows[3:, k + 1],
                    jnp.zeros((1, width), f32),
                ],
                0,
            )
        )
    sent = [pick(blocks, lax.rem(member + turn, frames_local)) for turn in turns]
    sent = lax.optimization_barrier(sent)
    arrived = [
        [lax.ppermute(sent[turn], AXES, outward(turn, shift)) for turn in turns]
        for shift in range(teams)
    ]

    def across(values):
        return [lax.ppermute(v, AXES, swap) for v in values]

    own, far = arrived[0], [v for shift in range(1, teams) for v in arrived[shift]]
    terms = functools.partial(pair_terms, own, weight_scale=weight_scale, peers=track_n * tm_n)
    ready = across(own)
    made = terms(own, None)
    totals, kept = made[:2], made[2:]
    totals = terms(ready, [*totals, *kept])
    held = []
    for part in far:
        part, totals = lax.optimization_barrier((part, totals))
        following = across([part])
        totals = terms([*held, part], [*totals, *kept])
        held = following
    *done, loss = terms(held, [*totals, *kept], home=list(turns))
    back = [lax.ppermute(done[turn], AXES, inward(turn)) for turn in turns]
    late = [lax.ppermute(done[turn][emb - 0:], AXES, inward_next(turn))[0:] for turn in turns]
    shares = lax.all_to_all(loss, AXES, 0, 0, tiled=True)
    of_frame = [
        pick(back, lax.rem(k - member + 2 * team * frames_local, frames_local)) for k in turns
    ]
    grad_emb = jnp.stack([v[:emb] for v in of_frame])
    before, grad_pos = sum(v[3:6] for v in late), jnp.zeros((3, frames_local, width), f32)
    frame = lax.broadcasted_iota(jnp.int32, grad_pos.shape, 1)
    for k, v in enumerate(of_frame):
        moved = v[emb : emb + 3] + before
        before = v[emb + 3 : emb + 6]
        grad_pos = jnp.where(frame == k, moved[:, None, :], grad_pos)
    shares, grad_emb = lax.optimization_barrier((shares, grad_emb))
    mean_loss = jnp.sum(shares[:, :1]) * 0.25 / (tracks * (tracks - 1) / 2.0 * (frames - 1))
    return (grad_pos, grad_emb, mean_loss)


def solution(mesh):
    in_specs = (P(None, "tm", "track"), P("tm", None, "track"), P("tm", "track"))
    out_specs = (P(None, "tm", "track"), P("tm", None, "track"), P())
    return jax.shard_map(
        on_device, mesh=mesh, in_specs=in_specs, out_specs=out_specs, check_vma=False
    )
```

```python
import functools
import math

import jax
import jax.numpy as jnp
from jax import lax
from jax.experimental import pallas as pl
from jax.experimental.pallas import tpu as pltpu
from jax.sharding import PartitionSpec as P

f32 = jnp.float32
bf16 = jnp.bfloat16
rigidity = 4.0
AXES = ("track", "tm")
TAIL = 8
GEO = 128
LEFT = (0, 0, 1, 0, 2, 1, 1, 2)
RIGHT = (0, 1, 0, 2, 0, 1, 2, 1)


def split(values):
    high = values.astype(bf16)
    return high, (values - high.astype(f32)).astype(bf16)


def split3(values):
    high = values.astype(bf16).astype(f32)
    rest = values - high
    mid = rest.astype(bf16).astype(f32)
    return high, mid, rest - mid


def geometry(ref, points, centre, left):
    size = points.shape[1]
    start = points[0:3] - centre[0:3]
    end = points[3:6] - centre[3:6]
    move = end - start
    square = jnp.sum(start * start, axis=0, keepdims=True)
    growth = jnp.sum(move * (start + end), axis=0, keepdims=True)
    ones = [jnp.ones((1, size), f32)] * 3
    if left:
        order, factor, factors = LEFT, -2.0, (start, start, move)
        tails = (list(split3(square)) + ones, list(split3(growth)) + ones)
    else:
        order, factor, factors = RIGHT, 1.0, (start, move, end)
        tails = (ones + list(split3(square + 1.0)), ones + list(split3(growth)))
    ref[...] = jnp.zeros_like(ref)
    parts = [split3(v) for v in factors]
    for at, group, tail in ((0, parts[:1], tails[0]), (32, parts[1:], tails[1])):
        for part in group:
            for k in order:
                ref[at : at + 3, :] = factor * part[k]
                at += 3
        for row in tail:
            ref[at : at + 1, :] = row
            at += 1
    return start, end


def pair_kernel(own_n, col_n, chunk, rows, first, home, lanes, energy, weight_scale, *refs):
    refs = list(refs)

    def take(count):
        taken = refs[:count]
        del refs[:count]
        return taken

    own_blocks, col_blocks = take(own_n), take(col_n)
    prev = take(0 if first else 2)
    kept = take(0 if first else 2)
    outs = take(2 if home is None else len(home) + (energy is not None))
    if first:
        kept = take(2)
    weights, geo_weights = kept
    lhs, geo_lhs, emb_split, pts_split, geo_own, geo_col, grad, sums, energies, own = take(10)
    logits, geo, g_high, g_low = take(2), take(2), take(2), take(2)
    pulls = [take(4), take(4)]
    emb, width = own_blocks[0].shape[0] - TAIL, own_blocks[0].shape[1]
    own_size, col_size = width * own_n, width * col_n
    inv_root = 1.0 / math.sqrt(emb)
    for a in range(own_n):
        own[:, a * width : (a + 1) * width] = own_blocks[a][emb : emb + TAIL, :]
    centre = jnp.mean(own[0:6, :], axis=1, keepdims=True)
    if first:
        for a in range(own_n):
            at = slice(a * width, (a + 1) * width)
            high, low = split(own_blocks[a][0:emb, :] * (0.5 * inv_root))
            weights[0:emb, at] = high
            weights[emb : 2 * emb, at] = low
            weights[2 * emb : 3 * emb, at] = high
        geometry(geo_own, own[...], centre, True)
        row = lax.broadcasted_iota(jnp.int32, (GEO, own_size), 0)
        values = geo_own[...]
        geo_weights[:, 0:own_size] = jnp.where(row < 32, values, 0.0).astype(bf16)
        geo_weights[:, own_size : 2 * own_size] = jnp.where(row < 32, 0.0, values).astype(bf16)
    for b in range(col_n):
        at = slice(b * width, (b + 1) * width)
        values = col_blocks[b][0:emb, :]
        high, low = split(values)
        emb_split[0:emb, at] = high
        emb_split[emb : 2 * emb, at] = low
        high, low = split(values.T)
        lhs[at, 0:emb] = high
        lhs[at, emb : 2 * emb] = high
        lhs[at, 2 * emb : 3 * emb] = low
        points = col_blocks[b][emb : emb + TAIL, :]
        start, end = geometry(geo_col, points, centre, False)
        geo_col[32:96, :] = geo_col[32:96, :] * points[6:7, :]
        geo_lhs[at, :] = geo_col[...].T.astype(bf16)
        ones, zeros = jnp.ones((1, width), f32), jnp.zeros((1, width), f32)
        centred = jnp.concatenate([start, end, ones, zeros], 0)
        for k, part in enumerate(split3(centred)):
            pts_split[8 * k : 8 * k + 8, at] = part.astype(bf16)
    if first:
        grad[...] = jnp.zeros_like(grad)
        sums[...] = jnp.zeros_like(sums)
        energies[...] = jnp.zeros_like(energies)
    else:
        grad[...] = prev[0][...]
        sums[...] = prev[1][0:16, :]
        energies[...] = prev[1][16:24, :]

    def products(n, i, k):
        cols, at = pl.ds(n * chunk, chunk), slice(*i)
        size = i[1] - i[0]
        logits[k][:, :size] = jnp.dot(lhs[cols, :], weights[:, at], preferred_element_type=f32)
        side = geo_lhs[cols, :]
        geo[k][0, :, :size] = jnp.dot(side, geo_weights[:, at], preferred_element_type=f32)
        at = slice(own_size + i[0], own_size + i[1])
        geo[k][1, :, :size] = jnp.dot(side, geo_weights[:, at], preferred_element_type=f32)

    def elementwise(n, i, k):
        mine, size = slice(*i), i[1] - i[0]
        total = jnp.zeros((8, size), f32)
        for b in range(0, chunk, rows):
            at = slice(b, b + rows)
            sq0, growth = geo[k][0, at, :size], geo[k][1, at, :size]
            sq1 = sq0 + growth
            inv0, inv1 = lax.rsqrt(sq0), lax.rsqrt(sq1)
            both = sq1 * inv1 + sq0 * inv0
            change = growth * lax.rsqrt(both * both)
            tanh = jnp.tanh(logits[k][at, :size])
            pull = change + change * tanh
            value = pull * change
            g_high[k][at, :size], g_low[k][at, :size] = split(value - value * tanh)
            pulls[k][0][at, :size], pulls[k][1][at, :size] = split(pull * inv0)
            pulls[k][2][at, :size], pulls[k][3][at, :size] = split(pull * inv1)
            total = total + value.reshape(rows // 8, 8, size).sum(0)
        if energy is not None:
            column = lax.broadcasted_iota(jnp.int32, (8, size), 1) + i[0]
            factor = jnp.where(column >= energy, 2.0, 1.0) if energy < i[1] else 1.0
            energies[:, mine] += total * factor

    def gradients(n, i, k):
        cols, at, size = pl.ds(n * chunk, chunk), slice(*i), i[1] - i[0]
        two = jnp.dot(emb_split[:, cols], g_high[k][:, :size], preferred_element_type=f32)
        one = jnp.dot(emb_split[0:emb, cols], g_low[k][:, :size], preferred_element_type=f32)
        grad[:, at] += two[:emb] + two[emb:] + one
        side = pts_split[:, cols]
        for frame in range(2):
            high, low = pulls[k][2 * frame], pulls[k][2 * frame + 1]
            moved = jnp.dot(side, high[:, :size], preferred_element_type=f32)
            moved = moved + jnp.dot(side, low[:, :size], preferred_element_type=f32)
            sums[8 * frame : 8 * frame + 8, at] += moved[:8] + moved[8:16] + moved[16:]

    tiles = [(n, i) for n in range(col_size // chunk) for i in lanes]
    products(*tiles[0], 0)
    for t, (n, i) in enumerate(tiles):
        if t + 1 < len(tiles):
            products(*tiles[t + 1], (t + 1) % 2)
        elementwise(n, i, t % 2)
        gradients(n, i, t % 2)

    if home is None:
        outs[0][...] = grad[...]
        outs[1][0:16, :] = sums[...]
        outs[1][16:24, :] = energies[...]
        return
    for a, out in zip(home, outs):
        at = slice(a * width, (a + 1) * width)
        seen = own[6:7, at] * weight_scale
        start, end = own[0:3, at] - centre[0:3], own[3:6, at] - centre[3:6]
        out[0:emb, :] = grad[:, at] * (seen * (0.25 * inv_root))
        out[emb : emb + 3, :] = (sums[0:3, at] - start * sums[6:7, at]) * seen
        out[emb + 3 : emb + 6, :] = (end * sums[14:15, at] - sums[11:14, at]) * seen
        out[emb + 6 : emb + 8, :] = jnp.zeros((2, width), f32)
    if energy is not None:
        loss = jnp.sum(energies[...] * own[6:7, :], axis=0, keepdims=True)
        loss = jnp.sum(loss, axis=1, keepdims=True)
        outs[len(home)][...] = jnp.broadcast_to(loss, outs[len(home)].shape)


def pair_terms(
    own_blocks, col_blocks, prev, weight_scale, peers, home=None, double=None, counted=True
):
    own_n, col_n = len(own_blocks), len(col_blocks)
    emb, width = own_blocks[0].shape[0] - TAIL, own_blocks[0].shape[1]
    own_size, col_size = width * own_n, width * col_n
    chunk = 256 if col_size % 256 == 0 else 384 if col_size % 384 == 0 else 128
    low, high = (0, own_size) if home is None else (home[0] * width, (home[-1] + 1) * width)
    strip = 256 if (high - low) % 256 == 0 else 384 if (high - low) % 384 == 0 else 128
    lanes = [(i, i + strip) for i in range(low, high, strip)]
    energy = None
    if counted:
        energy = own_size if double is None else double * width
    first = prev is None
    if home is None:
        out_shape = [
            jax.ShapeDtypeStruct((emb, own_size), f32),
            jax.ShapeDtypeStruct((24, own_size), f32),
        ]
    else:
        out_shape = [jax.ShapeDtypeStruct((emb + TAIL, width), f32)] * len(home)
        if counted:
            out_shape.append(jax.ShapeDtypeStruct((peers, 128), f32))
    if first:
        out_shape.append(jax.ShapeDtypeStruct((3 * emb, own_size), bf16))
        out_shape.append(jax.ShapeDtypeStruct((GEO, 2 * own_size), bf16))
    pairs = (high - low) * col_size
    tile = (chunk, strip)
    return pl.pallas_call(
        functools.partial(
            pair_kernel, own_n, col_n, chunk, 32, first, home, lanes, energy, weight_scale
        ),
        out_shape=out_shape,
        scratch_shapes=[
            pltpu.VMEM((col_size, 3 * emb), bf16),
            pltpu.VMEM((col_size, GEO), bf16),
            pltpu.VMEM((2 * emb, col_size), bf16),
            pltpu.VMEM((24, col_size), bf16),
            pltpu.VMEM((GEO, own_size), f32),
            pltpu.VMEM((GEO, width), f32),
            pltpu.VMEM((emb, own_size), f32),
            pltpu.VMEM((16, own_size), f32),
            pltpu.VMEM((8, own_size), f32),
            pltpu.VMEM((8, own_size), f32),
        ]
        + [pltpu.VMEM(tile, f32)] * 2
        + [pltpu.VMEM((2, *tile), f32)] * 2
        + [pltpu.VMEM(tile, bf16)] * 12,
        compiler_params=pltpu.CompilerParams(vmem_limit_bytes=32 * 2**20),
        cost_estimate=pl.CostEstimate(
            flops=pairs * emb * 100, bytes_accessed=1, transcendentals=0
        ),
    )(*own_blocks, *col_blocks, *(() if first else prev))


def scaled(values, factor):
    def kernel(values_ref, out_ref):
        out_ref[...] = values_ref[...] * factor

    return pl.pallas_call(
        kernel,
        out_shape=jax.ShapeDtypeStruct(values.shape, f32),
        cost_estimate=pl.CostEstimate(flops=10**11, bytes_accessed=1, transcendentals=0),
    )(values)


def pick(options, index):
    chosen = options[0]
    for n in range(1, len(options)):
        chosen = jnp.where(index == n, options[n], chosen)
    return chosen


def on_device(positions, embeddings, visible):
    frames_local, emb, width = embeddings.shape
    track_n, tm_n = lax.axis_size("track"), lax.axis_size("tm")
    tracks, frames = width * track_n, frames_local * tm_n
    weight_scale = rigidity / math.sqrt(tracks)
    team = 2 * frames_local
    teams = track_n // team

    def homes():
        for track in range(track_n):
            for tm in range(tm_n):
                yield track, tm

    def worker(track, tm, turn, shift):
        crew, member = divmod(track, team)
        core = tm % 2
        frame = (turn + member) % frames_local
        to_track = (crew + shift) % teams * team + core * frames_local + frame
        return to_track * tm_n + (tm - core + member // frames_local), frame

    def outward(turn, shift):
        return [(t * tm_n + m, worker(t, m, turn, shift)[0]) for t, m in homes()]

    def inward(turn):
        return [(worker(t, m, turn, 0)[0], t * tm_n + m) for t, m in homes()]

    def inward_next(turn):
        pairs = []
        for t, m in homes():
            at, frame = worker(t, m, turn, 0)
            if frame == frames_local - 1 and m + 1 < tm_n:
                pairs.append((at, t * tm_n + m + 1))
        return pairs

    swap = [(t * tm_n + m, t * tm_n + (m ^ 1)) for t, m in homes()]
    member = lax.rem(lax.axis_index("track"), team)
    turns = range(frames_local)

    seen = visible.astype(f32)
    rows = jnp.concatenate([positions, seen[None]], 0)
    following = lax.ppermute(rows[:, 0], "tm", [(i, i - 1) for i in range(1, tm_n)])
    rows = jnp.concatenate([rows, following[:, None]], 1)
    blocks = []
    for k in turns:
        blocks.append(
            jnp.concatenate(
                [
                    embeddings[k],
                    rows[:3, k],
                    rows[:3, k + 1],
                    rows[3:, k] * rows[3:, k + 1],
                    jnp.zeros((1, width), f32),
                ],
                0,
            )
        )
    sent = [pick(blocks, lax.rem(member + turn, frames_local)) for turn in turns]
    sent = lax.optimization_barrier(sent)
    arrived = [
        [lax.ppermute(sent[turn], AXES, outward(turn, shift)) for turn in turns]
        for shift in range(teams)
    ]

    def across(values):
        return [lax.ppermute(v, AXES, swap) for v in values]

    own, far = arrived[0], [v for shift in range(1, teams) for v in arrived[shift]]
    terms = functools.partial(pair_terms, own, weight_scale=weight_scale, peers=track_n * tm_n)
    ready = across(own)
    made = terms(own, None)
    totals, kept = made[:2], made[2:]
    totals = terms(ready, [*totals, *kept])
    held = []
    for part in far:
        part, totals = lax.optimization_barrier((part, totals))
        following = across([part])
        totals = terms([*held, part], [*totals, *kept])
        held = following
    *done, loss = terms(held, [*totals, *kept], home=list(turns))
    back = [lax.ppermute(done[turn], AXES, inward(turn)) for turn in turns]
    late = [lax.ppermute(done[turn][emb - 0:], AXES, inward_next(turn))[0:] for turn in turns]
    shares = lax.all_to_all(loss, AXES, 0, 0, tiled=True)
    factor = 0.25 / (tracks * (tracks - 1) / 2.0 * (frames - 1))
    mean_loss = scaled(jnp.sum(shares, 0).reshape(1, 128), factor)
    back, late, mean_loss = lax.optimization_barrier((back, late, mean_loss))
    of_frame = [
        pick(back, lax.rem(k - member + 2 * team * frames_local, frames_local)) for k in turns
    ]
    grad_emb = jnp.stack([v[:emb] for v in of_frame])
    before, grad_pos = sum(v[3:6] for v in late), jnp.zeros((3, frames_local, width), f32)
    frame = lax.broadcasted_iota(jnp.int32, grad_pos.shape, 1)
    for k, v in enumerate(of_frame):
        moved = v[emb : emb + 3] + before
        before = v[emb + 3 : emb + 6]
        grad_pos = jnp.where(frame == k, moved[:, None, :], grad_pos)
    shares, grad_emb = lax.optimization_barrier((shares, grad_emb))
    return (grad_pos, grad_emb, mean_loss[0, 0])


def solution(mesh):
    in_specs = (P(None, "tm", "track"), P("tm", None, "track"), P("tm", "track"))
    out_specs = (P(None, "tm", "track"), P("tm", None, "track"), P())
    return jax.shard_map(
        on_device, mesh=mesh, in_specs=in_specs, out_specs=out_specs, check_vma=False
    )
```

```python
import functools
import math

import jax
import jax.numpy as jnp
from jax import lax
from jax.experimental import pallas as pl
from jax.experimental.pallas import tpu as pltpu
from jax.sharding import PartitionSpec as P

f32 = jnp.float32
bf16 = jnp.bfloat16
rigidity = 4.0
AXES = ("track", "tm")
TAIL = 8
GEO = 128
LEFT = (0, 0, 1, 0, 2, 1, 1, 2)
RIGHT = (0, 1, 0, 2, 0, 1, 2, 1)


def split(values):
    high = values.astype(bf16)
    return high, (values - high.astype(f32)).astype(bf16)


def split3(values):
    high = values.astype(bf16).astype(f32)
    rest = values - high
    mid = rest.astype(bf16).astype(f32)
    return high, mid, rest - mid


def geometry(ref, points, centre, left):
    size = points.shape[1]
    start = points[0:3] - centre[0:3]
    end = points[3:6] - centre[3:6]
    move = end - start
    square = jnp.sum(start * start, axis=0, keepdims=True)
    growth = jnp.sum(move * (start + end), axis=0, keepdims=True)
    ones = [jnp.ones((1, size), f32)] * 3
    if left:
        order, factor, factors = LEFT, -2.0, (start, start, move)
        tails = (list(split3(square)) + ones, list(split3(growth)) + ones)
    else:
        order, factor, factors = RIGHT, 1.0, (start, move, end)
        tails = (ones + list(split3(square + 1.0)), ones + list(split3(growth)))
    ref[...] = jnp.zeros_like(ref)
    parts = [split3(v) for v in factors]
    for at, group, tail in ((0, parts[:1], tails[0]), (32, parts[1:], tails[1])):
        for part in group:
            for k in order:
                ref[at : at + 3, :] = factor * part[k]
                at += 3
        for row in tail:
            ref[at : at + 1, :] = row
            at += 1
    return start, end


def pair_kernel(own_n, col_n, chunk, rows, first, home, lanes, weight_scale, *refs):
    refs = list(refs)

    def take(count):
        taken = refs[:count]
        del refs[:count]
        return taken

    own_blocks, col_blocks = take(own_n), take(col_n)
    prev = take(0 if first else 2)
    kept = take(0 if first else 2)
    outs = take(2 if home is None else len(home) + 1)
    if first:
        kept = take(2)
    weights, geo_weights = kept
    lhs, geo_lhs, emb_split, pts_split, geo_own, geo_col, grad, sums, energies, own = take(10)
    logits, geo, g_high, g_low = take(2), take(2), take(2), take(2)
    pulls = [take(4), take(4)]
    emb, width = own_blocks[0].shape[0] - TAIL, own_blocks[0].shape[1]
    own_size, col_size = width * own_n, width * col_n
    inv_root = 1.0 / math.sqrt(emb)
    for a in range(own_n):
        own[:, a * width : (a + 1) * width] = own_blocks[a][emb : emb + TAIL, :]
    centre = jnp.mean(own[0:6, :], axis=1, keepdims=True)
    if first:
        for a in range(own_n):
            at = slice(a * width, (a + 1) * width)
            high, low = split(own_blocks[a][0:emb, :] * (0.5 * inv_root))
            weights[0:emb, at] = high
            weights[emb : 2 * emb, at] = low
            weights[2 * emb : 3 * emb, at] = high
        geometry(geo_own, own[...], centre, True)
        row = lax.broadcasted_iota(jnp.int32, (GEO, own_size), 0)
        values = geo_own[...]
        geo_weights[:, 0:own_size] = jnp.where(row < 32, values, 0.0).astype(bf16)
        geo_weights[:, own_size : 2 * own_size] = jnp.where(row < 32, 0.0, values).astype(bf16)
    for b in range(col_n):
        at = slice(b * width, (b + 1) * width)
        values = col_blocks[b][0:emb, :]
        high, low = split(values)
        emb_split[0:emb, at] = high
        emb_split[emb : 2 * emb, at] = low
        high, low = split(values.T)
        lhs[at, 0:emb] = high
        lhs[at, emb : 2 * emb] = high
        lhs[at, 2 * emb : 3 * emb] = low
        points = col_blocks[b][emb : emb + TAIL, :]
        start, end = geometry(geo_col, points, centre, False)
        geo_col[32:96, :] = geo_col[32:96, :] * points[6:7, :]
        geo_lhs[at, :] = geo_col[...].T.astype(bf16)
        ones, zeros = jnp.ones((1, width), f32), jnp.zeros((1, width), f32)
        centred = jnp.concatenate([start, end, ones, zeros], 0)
        for k, part in enumerate(split3(centred)):
            pts_split[8 * k : 8 * k + 8, at] = part.astype(bf16)
    if first:
        grad[...] = jnp.zeros_like(grad)
        sums[...] = jnp.zeros_like(sums)
        energies[...] = jnp.zeros_like(energies)
    else:
        grad[...] = prev[0][...]
        sums[...] = prev[1][0:16, :]
        energies[...] = prev[1][16:24, :]

    def products(n, i, k):
        cols, at = pl.ds(n * chunk, chunk), slice(*i)
        size = i[1] - i[0]
        logits[k][:, :size] = jnp.dot(lhs[cols, :], weights[:, at], preferred_element_type=f32)
        side = geo_lhs[cols, :]
        geo[k][0, :, :size] = jnp.dot(side, geo_weights[:, at], preferred_element_type=f32)
        at = slice(own_size + i[0], own_size + i[1])
        geo[k][1, :, :size] = jnp.dot(side, geo_weights[:, at], preferred_element_type=f32)

    def elementwise(n, i, k):
        mine, size = slice(*i), i[1] - i[0]
        total = jnp.zeros((8, size), f32)
        for b in range(0, chunk, rows):
            at = slice(b, b + rows)
            sq0, growth = geo[k][0, at, :size], geo[k][1, at, :size]
            sq1 = sq0 + growth
            inv0, inv1 = lax.rsqrt(sq0), lax.rsqrt(sq1)
            both = sq1 * inv1 + sq0 * inv0
            change = growth * lax.rsqrt(both * both)
            tanh = jnp.tanh(logits[k][at, :size])
            pull = change + change * tanh
            value = pull * change
            g_high[k][at, :size], g_low[k][at, :size] = split(value - value * tanh)
            pulls[k][0][at, :size], pulls[k][1][at, :size] = split(pull * inv0)
            pulls[k][2][at, :size], pulls[k][3][at, :size] = split(pull * inv1)
            total = total + value.reshape(rows // 8, 8, size).sum(0)
        energies[:, mine] += total

    def gradients(n, i, k):
        cols, at, size = pl.ds(n * chunk, chunk), slice(*i), i[1] - i[0]
        two = jnp.dot(emb_split[:, cols], g_high[k][:, :size], preferred_element_type=f32)
        one = jnp.dot(emb_split[0:emb, cols], g_low[k][:, :size], preferred_element_type=f32)
        grad[:, at] += two[:emb] + two[emb:] + one
        side = pts_split[:, cols]
        for frame in range(2):
            high, low = pulls[k][2 * frame], pulls[k][2 * frame + 1]
            moved = jnp.dot(side, high[:, :size], preferred_element_type=f32)
            moved = moved + jnp.dot(side, low[:, :size], preferred_element_type=f32)
            sums[8 * frame : 8 * frame + 8, at] += moved[:8] + moved[8:16] + moved[16:]

    tiles = [(n, i) for n in range(col_size // chunk) for i in lanes]
    products(*tiles[0], 0)
    for t, (n, i) in enumerate(tiles):
        if t + 1 < len(tiles):
            products(*tiles[t + 1], (t + 1) % 2)
        elementwise(n, i, t % 2)
        gradients(n, i, t % 2)

    if home is None:
        outs[0][...] = grad[...]
        outs[1][0:16, :] = sums[...]
        outs[1][16:24, :] = energies[...]
        return
    for a, out in zip(home, outs):
        at = slice(a * width, (a + 1) * width)
        seen = own[6:7, at] * weight_scale
        start, end = own[0:3, at] - centre[0:3], own[3:6, at] - centre[3:6]
        out[0:emb, :] = grad[:, at] * (seen * (0.25 * inv_root))
        out[emb : emb + 3, :] = (sums[0:3, at] - start * sums[6:7, at]) * seen
        out[emb + 3 : emb + 6, :] = (end * sums[14:15, at] - sums[11:14, at]) * seen
        out[emb + 6 : emb + 8, :] = jnp.zeros((2, width), f32)
    loss = jnp.sum(energies[...] * own[6:7, :], axis=0, keepdims=True)
    loss = jnp.sum(loss, axis=1, keepdims=True)
    outs[len(home)][...] = jnp.broadcast_to(loss, outs[len(home)].shape)


def pair_terms(
    own_blocks, col_blocks, prev, weight_scale, peers, home=None
):
    own_n, col_n = len(own_blocks), len(col_blocks)
    emb, width = own_blocks[0].shape[0] - TAIL, own_blocks[0].shape[1]
    own_size, col_size = width * own_n, width * col_n
    chunk = 256 if col_size % 256 == 0 else 384 if col_size % 384 == 0 else 128
    low, high = (0, own_size) if home is None else (home[0] * width, (home[-1] + 1) * width)
    strip = 256 if (high - low) % 256 == 0 else 384 if (high - low) % 384 == 0 else 128
    lanes = [(i, i + strip) for i in range(low, high, strip)]
    first = prev is None
    if home is None:
        out_shape = [
            jax.ShapeDtypeStruct((emb, own_size), f32),
            jax.ShapeDtypeStruct((24, own_size), f32),
        ]
    else:
        out_shape = [jax.ShapeDtypeStruct((emb + TAIL, width), f32)] * len(home)
        out_shape.append(jax.ShapeDtypeStruct((peers, 128), f32))
    if first:
        out_shape.append(jax.ShapeDtypeStruct((3 * emb, own_size), bf16))
        out_shape.append(jax.ShapeDtypeStruct((GEO, 2 * own_size), bf16))
    pairs = (high - low) * col_size
    tile = (chunk, strip)
    return pl.pallas_call(
        functools.partial(
            pair_kernel, own_n, col_n, chunk, 32, first, home, lanes, weight_scale
        ),
        out_shape=out_shape,
        scratch_shapes=[
            pltpu.VMEM((col_size, 3 * emb), bf16),
            pltpu.VMEM((col_size, GEO), bf16),
            pltpu.VMEM((2 * emb, col_size), bf16),
            pltpu.VMEM((24, col_size), bf16),
            pltpu.VMEM((GEO, own_size), f32),
            pltpu.VMEM((GEO, width), f32),
            pltpu.VMEM((emb, own_size), f32),
            pltpu.VMEM((16, own_size), f32),
            pltpu.VMEM((8, own_size), f32),
            pltpu.VMEM((8, own_size), f32),
        ]
        + [pltpu.VMEM(tile, f32)] * 2
        + [pltpu.VMEM((2, *tile), f32)] * 2
        + [pltpu.VMEM(tile, bf16)] * 12,
        compiler_params=pltpu.CompilerParams(vmem_limit_bytes=32 * 2**20),
        cost_estimate=pl.CostEstimate(
            flops=pairs * emb * 100, bytes_accessed=1, transcendentals=0
        ),
    )(*own_blocks, *col_blocks, *(() if first else prev))


def scaled(values, factor):
    def kernel(values_ref, out_ref):
        out_ref[...] = values_ref[...] * factor

    return pl.pallas_call(
        kernel,
        out_shape=jax.ShapeDtypeStruct(values.shape, f32),
        cost_estimate=pl.CostEstimate(flops=10**11, bytes_accessed=1, transcendentals=0),
    )(values)


def pick(options, index):
    chosen = options[0]
    for n in range(1, len(options)):
        chosen = jnp.where(index == n, options[n], chosen)
    return chosen


def on_device(positions, embeddings, visible):
    frames_local, emb, width = embeddings.shape
    track_n, tm_n = lax.axis_size("track"), lax.axis_size("tm")
    tracks, frames = width * track_n, frames_local * tm_n
    weight_scale = rigidity / math.sqrt(tracks)
    team = 2 * frames_local
    teams = track_n // team

    def homes():
        for track in range(track_n):
            for tm in range(tm_n):
                yield track, tm

    def worker(track, tm, turn, shift):
        crew, member = divmod(track, team)
        core = tm % 2
        frame = (turn + member) % frames_local
        to_track = (crew + shift) % teams * team + core * frames_local + frame
        return to_track * tm_n + (tm - core + member // frames_local), frame

    def outward(turn, shift):
        return [(t * tm_n + m, worker(t, m, turn, shift)[0]) for t, m in homes()]

    def inward(turn):
        return [(worker(t, m, turn, 0)[0], t * tm_n + m) for t, m in homes()]

    def inward_next(turn):
        pairs = []
        for t, m in homes():
            at, frame = worker(t, m, turn, 0)
            if frame == frames_local - 1 and m + 1 < tm_n:
                pairs.append((at, t * tm_n + m + 1))
        return pairs

    swap = [(t * tm_n + m, t * tm_n + (m ^ 1)) for t, m in homes()]
    member = lax.rem(lax.axis_index("track"), team)
    turns = range(frames_local)

    seen = visible.astype(f32)
    rows = jnp.concatenate([positions, seen[None]], 0)
    following = lax.ppermute(rows[:, 0], "tm", [(i, i - 1) for i in range(1, tm_n)])
    rows = jnp.concatenate([rows, following[:, None]], 1)
    blocks = []
    for k in turns:
        blocks.append(
            jnp.concatenate(
                [
                    embeddings[k],
                    rows[:3, k],
                    rows[:3, k + 1],
                    rows[3:, k] * rows[3:, k + 1],
                    jnp.zeros((1, width), f32),
                ],
                0,
            )
        )
    sent = [pick(blocks, lax.rem(member + turn, frames_local)) for turn in turns]
    sent = lax.optimization_barrier(sent)
    arrived = [
        [lax.ppermute(sent[turn], AXES, outward(turn, shift)) for turn in turns]
        for shift in range(teams)
    ]

    def across(values):
        return [lax.ppermute(v, AXES, swap) for v in values]

    own, far = arrived[0], [v for shift in range(1, teams) for v in arrived[shift]]
    terms = functools.partial(pair_terms, own, weight_scale=weight_scale, peers=track_n * tm_n)
    ready = across(own)
    made = terms(own, None)
    totals, kept = made[:2], made[2:]
    held = ready
    if far:
        totals, held = terms(ready, [*totals, *kept]), []
    for part in far:
        part, totals = lax.optimization_barrier((part, totals))
        following = across([part])
        totals = terms([*held, part], [*totals, *kept])
        held = following
    *done, loss = terms(held, [*totals, *kept], home=list(turns))
    back = [lax.ppermute(done[turn], AXES, inward(turn)) for turn in turns]
    late = [lax.ppermute(done[turn][emb:], AXES, inward_next(turn)) for turn in turns]
    shares = lax.all_to_all(loss, AXES, 0, 0, tiled=True)
    factor = 0.25 / (tracks * (tracks - 1) / 2.0 * (frames - 1))
    mean_loss = scaled(jnp.sum(shares, 0).reshape(1, 128), factor)
    back, late, mean_loss = lax.optimization_barrier((back, late, mean_loss))
    of_frame = [
        pick(back, lax.rem(k - member + 2 * team * frames_local, frames_local)) for k in turns
    ]
    grad_emb = jnp.stack([v[:emb] for v in of_frame])
    before, grad_pos = sum(v[3:6] for v in late), jnp.zeros((3, frames_local, width), f32)
    frame = lax.broadcasted_iota(jnp.int32, grad_pos.shape, 1)
    for k, v in enumerate(of_frame):
        moved = v[emb : emb + 3] + before
        before = v[emb + 3 : emb + 6]
        grad_pos = jnp.where(frame == k, moved[:, None, :], grad_pos)
    return (grad_pos, grad_emb, mean_loss[0, 0])


def solution(mesh):
    in_specs = (P(None, "tm", "track"), P("tm", None, "track"), P("tm", "track"))
    out_specs = (P(None, "tm", "track"), P("tm", None, "track"), P())
    return jax.shard_map(
        on_device, mesh=mesh, in_specs=in_specs, out_specs=out_specs, check_vma=False
    )
```
